128 devices in a mesh: rows: 8 (over x, core), cols: 16 (over y, z).
Axes of the slice: x: 4, y: 4, z: 4, core: 2. Of those that a mesh axis runs over, the one named last changes fastest.
Arguments:
- momentum: float32 [8192, 26624], P('rows', 'cols'), may hold values from -40 to 40
- grad: bfloat16 [8192, 26624], P('rows', 'cols'), may hold values from -20 to 20
- q_basis: bfloat16 [26624, 512], P('cols'), may hold values from -6 to 6
Outputs:
- mom_next: float32 [8192, 26624], P('rows', 'cols')
- q_next: bfloat16 [26624, 512], P('cols')
- update: bfloat16 [8192, 26624], P('rows', 'cols')
The draws below stay inside these ranges and needn't reach their ends.
All inputs are finite; a program needn't handle non-finite values.
Results may differ from the reference program's by a relative error of at most 0.0029.
Values sent between devices are 32-bit elements; how exact they have to be, the bound alone decides.
A program may use at most 128 MiB of HBM per device.

```python
import math
import jax
import jax.numpy as jnp
from jax import lax

ROWS = 8192
COLS = 26624
RANK = 512


def column_scales(key):
    position = jnp.arange(COLS, dtype=jnp.float32) / (COLS - 1)
    spread = jax.random.uniform(key, (COLS,), jnp.float32, 0.0, 1.0)
    return jnp.exp(position * math.log(3.0) + spread * math.log(10.0)) / 5.0


def draw_momentum(key, part):
    scales = column_scales(key)
    key = jax.random.fold_in(key, 11)
    value = jnp.clip(jax.random.normal(key, (ROWS, COLS), jnp.float32), -4.0, 4.0) * scales
    return value


def draw_grad(key, part):
    scales = column_scales(key)
    key = jax.random.fold_in(key, 23)
    value = 0.5 * jnp.clip(jax.random.normal(key, (ROWS, COLS), jnp.float32), -4.0, 4.0) * scales
    return value.astype(jnp.bfloat16)


def shard_levels(stream_key, dims, cuts, low, high):
    level = 1.0
    for dim, parts in cuts:
        draws = jax.random.uniform(jax.random.fold_in(jax.random.fold_in(stream_key, 6), dim), (parts,), jnp.float32, low / len(cuts), high / len(cuts))
        level = level * jnp.repeat(jnp.exp(draws), dims[dim] // parts).reshape((-1,) + (1,) * (len(dims) - 1 - dim))
    return level


def bell_draw(rng, shape, width, limit, shards=(), kind=jnp.bfloat16):
    array = jax.random.normal(rng, shape, jnp.float32) * width
    if len(shards) > 0:
        array = shard_levels(rng, shape, shards, -0.22, 0.18) * array
    return jnp.clip(array, min=-limit, max=limit).astype(kind)


def setup_inputs(seed: int = 0) -> dict:
    arg_keys = jax.random.split(jax.random.key(seed), 4)
    return {
        "momentum": draw_momentum(jax.random.fold_in(arg_keys[3], 71), 0),
        "grad": draw_grad(jax.random.fold_in(arg_keys[3], 71), 0),
        "q_basis": bell_draw(arg_keys[2], (COLS, RANK), 1.0, 6.0, ((0, 16),)),
    }


feedback_rate = 0.05
epsilon = 1e-05

def exact_dot(left, right_side):
    return jnp.dot(left.astype(jnp.float32), right_side.astype(jnp.float32), precision=lax.Precision.HIGHEST, preferred_element_type=jnp.float32)

def orthonormal(matrix):
    gram_total = exact_dot(matrix.T, matrix)
    low_factor = jnp.linalg.cholesky(gram_total)
    return jax.scipy.linalg.solve_triangular(low_factor, matrix.T, lower=True).T

def reference(momentum, grad, q_basis):
    merged = momentum + grad.astype(jnp.float32)
    projected = exact_dot(merged, q_basis.astype(jnp.float32))
    orth_basis = orthonormal(projected)
    right_factor = lax.dot_general(merged.astype(jnp.float32), orth_basis.astype(jnp.float32), (((0,), (0,)), ((), ())), precision=lax.Precision.HIGHEST, preferred_element_type=jnp.float32)
    mom_next = merged - feedback_rate * exact_dot(orth_basis, right_factor.T)
    column_sq = lax.optimization_barrier(jnp.mean(right_factor * right_factor, axis=0))
    q_float = right_factor * lax.rsqrt(column_sq + epsilon)
    update = (jnp.sqrt(jnp.float32(ROWS) / RANK) * exact_dot(orth_basis, q_float.T)).astype(jnp.bfloat16)
    return (mom_next, q_float.astype(jnp.bfloat16), update)
```

```python
import functools

import jax
import jax.numpy as jnp
from jax import lax
from jax.experimental import pallas as pl
from jax.experimental.pallas import tpu as pltpu
from jax.sharding import PartitionSpec as P

ROWS = 8192
COLS = 26624
RANK = 512
feedback_rate = 0.05
epsilon = 1e-05

R = 1024
C = 1664
B = 128
MESH = pl.DeviceIdType.MESH
f32 = jnp.float32
bf16 = jnp.bfloat16
NN = (((1,), (0,)), ((), ()))
NT = (((1,), (1,)), ((), ()))


def mm(a, b, dims):
    return lax.dot_general(a, b, dims, preferred_element_type=f32)


def mm6(a, b, dims):
    return lax.dot_general(a, b, dims, precision=lax.Precision.HIGHEST, preferred_element_type=f32)


def split(a):
    hi = a.astype(bf16)
    return hi, (a - hi.astype(f32)).astype(bf16)


def mm3(a, b, dims):
    return mm(a[0], b[0], dims) + (mm(a[0], b[1], dims) + mm(a[1], b[0], dims))


def tree(terms):
    while len(terms) > 1:
        terms = [a + b for a, b in zip(terms[::2], terms[1::2])]
    return terms[0]


def inverse_factor(block):
    lane = lax.broadcasted_iota(jnp.int32, (8, B), 1)
    sub = lax.broadcasted_iota(jnp.int32, (8, B), 0)
    rows = [block[8 * v : 8 * v + 8, :] for v in range(16)]

    def row(x, l):
        return jnp.broadcast_to(x[l : l + 1, :], (8, B))

    def column(x, l):
        return jnp.broadcast_to(x[:, l : l + 1], (8, B))

    out = []
    for g in range(16):
        o = 8 * g
        active = (lane >= o) & (lane < o + 8)
        c = [column(rows[g], o + m) for m in range(8)]
        e = jnp.where(active, jnp.where(lane - o == sub, 1.0, 0.0), rows[g])
        e_row = [row(e, m) for m in range(8)]
        low = [jnp.where(sub == m, 1.0, 0.0) for m in range(8)]
        pivots = jnp.ones((8, B), f32)
        for l in range(8):
            here = sub == l
            r = [row(c[m], l) for m in range(8)]
            inverse = 1.0 / r[l]
            pivots = jnp.where(here, c[l], pivots)
            for m in range(l):
                low[m] = jnp.where(here, c[m], low[m])
            factor = jnp.where(here, -1.0, c[l])
            for m in range(8):
                if m != l:
                    c[m] = jnp.where(here, 0.0, c[m]) - (factor * r[m]) * inverse
            c[l] = -(factor * inverse)
        t = tree([low[m] * e_row[m] for m in range(8)])
        out.append(lax.rsqrt(pivots) * jnp.where(lane < o + 8, t, 0.0))
        if g == 15:
            break
        w = tree([c[m] * e_row[m] for m in range(8)])
        w_row = [row(w, m) for m in range(8)]
        for v in range(g + 1, 16):
            step = tree([column(rows[v], o + m) * w_row[m] for m in range(8)])
            rows[v] = jnp.where(active, 0.0, rows[v]) - step
    return jnp.concatenate(out, axis=0)


def factor_step(k, gram, inv):
    o, p = B * k, B * (k + 1)
    diagonal = inverse_factor(gram[o:p, o:p])
    if k > 0:
        inv[o:p, 0:o] = mm6(diagonal, inv[o:p, 0:o], NN)
    inv[o:p, o:p] = diagonal
    if k < 3:
        low = mm6(gram[p:, o:p], diagonal, NT)
        gram[p:, p:] = gram[p:, p:] - mm6(low, low, NT)
        inv[p:, 0:p] = inv[p:, 0:p] - mm6(low, inv[o:p, 0:p], NN)


P1, P2, P3, P4 = 0, 6, 12, 18
G0, G1, G2, G3 = 24, 25, 28, 31
W0, W1, W2, W3 = 32, 33, 36, 39
S1, S2 = 40, 43
N_MSG = 46


def sum_kernel(
    mom_hbm, grad_hbm, q_ref,
    p_ref, inv_ref, rt_ref, scale_ref,
    mom, grad, hi, lo, part, recv1, mid, recv2, pt_hi, pt_lo,
    gram, g_recv0, g_recv1, wt, w_recv0, w_recv1, w_sum, col, col_recv,
    load_sem, send_sem, recv_sem,
):
    row, column = lax.axis_index("rows"), lax.axis_index("cols")
    x, core = row // 2, row % 2
    y, z = column // 4, column % 4

    def at_x(d):
        return (((x + d) % 4) * 2 + core, column)

    def at_y(d):
        return (row, ((y + d) % 4) * 4 + z)

    def at_z(d):
        return (row, y * 4 + (z + d) % 4)

    other_core = (x * 2 + 1 - core, column)

    loads = []
    for i in range(4):
        rows = pl.ds(256 * i, 256)
        pair = [
            pltpu.make_async_copy(mom_hbm.at[rows], mom.at[rows], load_sem.at[2 * i]),
            pltpu.make_async_copy(grad_hbm.at[rows], grad.at[rows], load_sem.at[2 * i + 1]),
        ]
        for copy in pair:
            copy.start()
        loads.append(pair)

    barrier = pltpu.get_barrier_semaphore()
    peers = [f(d) for f in (at_x, at_y, at_z) for d in (1, 2, 3)] + [other_core]
    for peer in peers:
        pl.semaphore_signal(barrier, inc=1, device_id=peer, device_id_type=MESH)
    pl.semaphore_wait(barrier, len(peers))

    def send(number, src, dst, peer):
        copy = pltpu.make_async_remote_copy(
            src_ref=src, dst_ref=dst, send_sem=send_sem.at[number], recv_sem=recv_sem.at[number],
            device_id=peer, device_id_type=MESH,
        )
        copy.start()
        return copy

    started = []

    def finish(copies):
        for copy in copies:
            copy.wait_recv()
        started.extend(copies)

    for i in range(4):
        for copy in loads[i]:
            copy.wait()

        @pl.loop(0, 8)
        def _(j):
            rows = pl.ds(pl.multiple_of(256 * i + 32 * j, 32), 32)
            top, rest = split(mom[rows, :] + grad[rows, :].astype(f32))
            hi[rows, :] = top
            lo[rows, :] = rest

    def at_first(h):
        return at_y if h == 0 else at_z

    def at_second(h):
        return at_z if h == 0 else at_y

    first, second = (y, z), (z, y)

    copies = []
    for d in (2, 1, 3, 0):
        for h in range(2):
            block = (first[h] + d) % 4
            rows = pl.ds(pl.multiple_of(block * 256, 256), 256)
            qh = q_ref[:, 256 * h : 256 * h + 256]
            part[h, rows, :] = mm(hi[rows, :], qh, NN) + mm(lo[rows, :], qh, NN)
            if d:
                copies.append(
                    send(P1 + 3 * h + d - 1, part.at[h, rows], recv1.at[h, d - 1], at_first(h)(d))
                )
    finish(copies)
    copies = []
    for h in range(2):
        rows = pl.ds(pl.multiple_of(first[h] * 256, 256), 256)
        mid[h] = (part[h, rows, :] + recv1[h, 0]) + (recv1[h, 1] + recv1[h, 2])
        for d in (2, 1, 3):
            rows = pl.ds(pl.multiple_of(((second[h] + d) % 4) * 64, 64), 64)
            copies.append(
                send(P2 + 3 * h + d - 1, mid.at[h, rows], recv2.at[h, d - 1], at_second(h)(d))
            )
    finish(copies)
    copies = []
    for h in range(2):
        rows = pl.ds(pl.multiple_of(second[h] * 64, 64), 64)
        mine = pl.ds(pl.multiple_of(first[h] * 256 + second[h] * 64, 64), 64)
        p_ref[h, mine, :] = (mid[h, rows, :] + recv2[h, 0]) + (recv2[h, 1] + recv2[h, 2])
        for d in (2, 1, 3):
            copies.append(
                send(P3 + 3 * h + d - 1, p_ref.at[h, mine], p_ref.at[h, mine], at_second(h)(d))
            )
    finish(copies)
    copies = []
    for h in range(2):
        mine = pl.ds(pl.multiple_of(first[h] * 256, 256), 256)
        for d in (2, 1, 3):
            copies.append(
                send(P4 + 3 * h + d - 1, p_ref.at[h, mine], p_ref.at[h, mine], at_first(h)(d))
            )
    finish(copies)

    for h in range(2):
        for i in range(4):
            t = p_ref[h, 256 * i : 256 * i + 256, :].T
            top, rest = split(t)
            pt_hi[256 * h : 256 * h + 256, 256 * i : 256 * i + 256] = top
            pt_lo[256 * h : 256 * h + 256, 256 * i : 256 * i + 256] = rest
    gram[...] = mm(pt_lo[...], pt_lo[...], NT) + mm3(
        (pt_hi[...], pt_lo[...]), (pt_hi[...], pt_lo[...]), NT
    )
    ours = pl.ds(pl.multiple_of(core * 256, 256), 256)
    theirs = pl.ds(pl.multiple_of((1 - core) * 256, 256), 256)
    g0 = send(G0, gram.at[theirs], g_recv0, other_core)

    def product(half):
        @pl.loop(0, 2)
        def _(j):
            rows = pl.ds(pl.multiple_of(half * 256 + 128 * j, 128), 128)
            wt[rows, :] = mm3((pt_hi[rows, :], pt_lo[rows, :]), (hi[...], lo[...]), NN)

    product(1 - core)
    w0 = send(W0, wt.at[theirs], w_recv0, other_core)
    finish([g0])
    gram[ours, :] = gram[ours, :] + g_recv0[...]

    def slab(i):
        return pl.ds(pl.multiple_of(core * 256 + i * 64, 64), 64)

    g1 = [send(G1 + d - 1, gram.at[slab((x + d) % 4)], g_recv1.at[d - 1], at_x(d)) for d in (2, 1, 3)]
    product(core)
    finish(g1)
    mine = slab(x)
    inv_ref[mine, :] = (gram[mine, :] + g_recv1[0]) + (g_recv1[1] + g_recv1[2])
    g2 = [send(G2 + d - 1, inv_ref.at[mine], inv_ref.at[mine], at_x(d)) for d in (2, 1, 3)]
    finish([w0])
    wt[ours, :] = wt[ours, :] + w_recv0[...]
    finish(g2)
    g3 = send(G3, inv_ref.at[ours], inv_ref.at[ours], other_core)
    w1 = [send(W1 + d - 1, wt.at[slab((x + d) % 4)], w_recv1.at[d - 1], at_x(d)) for d in (2, 1, 3)]
    finish([g3])
    settled = [g0, g3] + g1 + g2
    for copy in settled:
        copy.wait_send()

    gram[...] = inv_ref[...]
    inv_ref[...] = jnp.zeros((RANK, RANK), f32)
    factor_step(0, gram, inv_ref)
    factor_step(1, gram, inv_ref)
    finish(w1)
    w_sum[mine, :] = (wt[mine, :] + w_recv1[0]) + (w_recv1[1] + w_recv1[2])
    w2 = [send(W2 + d - 1, w_sum.at[mine], w_sum.at[mine], at_x(d)) for d in (2, 1, 3)]
    factor_step(2, gram, inv_ref)
    factor_step(3, gram, inv_ref)
    finish(w2)
    w3 = send(W3, w_sum.at[ours], w_sum.at[ours], other_core)
    finish([w3])

    inv_pair = split(inv_ref[...])
    squares = jnp.zeros((RANK, B), f32)
    for j in range(13):
        lanes = slice(B * j, B * j + B)
        r = mm3(inv_pair, split(w_sum[:, lanes]), NN)
        rt_ref[:, lanes] = r
        squares = squares + r * r
    col[0] = mm6(jnp.ones((8, B), f32), squares, NT)
    copies = [send(S1 + d - 1, col.at[0], col_recv.at[0, d - 1], at_y(d)) for d in (2, 1, 3)]
    finish(copies)
    col[1] = (col[0] + col_recv[0, 0]) + (col_recv[0, 1] + col_recv[0, 2])
    copies = [send(S2 + d - 1, col.at[1], col_recv.at[1, d - 1], at_z(d)) for d in (2, 1, 3)]
    finish(copies)
    total = (col[1] + col_recv[1, 0]) + (col_recv[1, 1] + col_recv[1, 2])
    scale_ref[...] = lax.rsqrt(total * (1.0 / COLS) + epsilon)
    for copy in started:
        if not any(copy is other for other in settled):
            copy.wait_send()


def sums(momentum, grad, q_basis):
    vmem = pl.BlockSpec(memory_space=pltpu.VMEM)
    hbm = pl.BlockSpec(memory_space=pl.ANY)
    return pl.pallas_call(
        sum_kernel,
        out_shape=[
            jax.ShapeDtypeStruct((2, R, 256), f32),
            jax.ShapeDtypeStruct((RANK, RANK), f32),
            jax.ShapeDtypeStruct((RANK, C), f32),
            jax.ShapeDtypeStruct((8, RANK), f32),
        ],
        in_specs=[hbm, hbm, vmem],
        out_specs=[vmem] * 4,
        scratch_shapes=[
            pltpu.VMEM((R, C), f32),
            pltpu.VMEM((R, C), bf16),
            pltpu.VMEM((R, C), bf16),
            pltpu.VMEM((R, C), bf16),
            pltpu.VMEM((2, R, 256), f32),
            pltpu.VMEM((2, 3, 256, 256), f32),
            pltpu.VMEM((2, 256, 256), f32),
            pltpu.VMEM((2, 3, 64, 256), f32),
            pltpu.VMEM((RANK, R), bf16),
            pltpu.VMEM((RANK, R), bf16),
            pltpu.VMEM((RANK, RANK), f32),
            pltpu.VMEM((256, RANK), f32),
            pltpu.VMEM((3, 64, RANK), f32),
            pltpu.VMEM((RANK, C), f32),
            pltpu.VMEM((256, C), f32),
            pltpu.VMEM((3, 64, C), f32),
            pltpu.VMEM((RANK, C), f32),
            pltpu.VMEM((2, 8, RANK), f32),
            pltpu.VMEM((2, 3, 8, RANK), f32),
            pltpu.SemaphoreType.DMA((8,)),
            pltpu.SemaphoreType.DMA((N_MSG,)),
            pltpu.SemaphoreType.DMA((N_MSG,)),
        ],
        compiler_params=pltpu.CompilerParams(
            collective_id=0, has_side_effects=True, vmem_limit_bytes=58 << 20
        ),
        name="sums",
    )(momentum, grad, q_basis)


def output_kernel(mom, grad, p_ref, inv_ref, rt_ref, scale_ref, mom_out, q_out, update_out, r_hi, r_lo, i_hi, i_lo):
    scale = scale_ref[0:1, :]

    @pl.when(pl.program_id(0) == 0)
    def _():
        i_hi[...], i_lo[...] = split(inv_ref[...])
        for j in range(13):
            lanes = slice(B * j, B * j + B)
            r = rt_ref[:, lanes]
            r_hi[:, lanes], r_lo[:, lanes] = split(r)
            q_out[lanes, :] = (r.T * scale).astype(bf16)

    p = jnp.concatenate([p_ref[0], p_ref[1]], axis=1)
    orth = mm3(split(p), (i_hi[...], i_lo[...]), NT)
    orth_hi = (orth * feedback_rate).astype(bf16)
    scaled = split(orth * (scale * (float(ROWS) / RANK) ** 0.5))
    mom_out[...] = mom[...] + grad[...].astype(f32) - mm(orth_hi, r_hi[...], NN)
    update_out[...] = mm3(scaled, (r_hi[...], r_lo[...]), NN).astype(bf16)


def outputs(momentum, grad, p, inv, rt, scale):
    rows = 128
    whole = lambda *shape: pl.BlockSpec(shape, lambda i: (0,) * len(shape))
    slab = pl.BlockSpec((rows, C), lambda i: (i, 0))
    return pl.pallas_call(
        output_kernel,
        grid=(R // rows,),
        out_shape=[
            jax.ShapeDtypeStruct((R, C), f32),
            jax.ShapeDtypeStruct((C, RANK), bf16),
            jax.ShapeDtypeStruct((R, C), bf16),
        ],
        in_specs=[
            slab, slab, pl.BlockSpec((2, rows, 256), lambda i: (0, i, 0)),
            whole(RANK, RANK), whole(RANK, C), whole(8, RANK),
        ],
        out_specs=[slab, whole(C, RANK), slab],
        scratch_shapes=[
            pltpu.VMEM((RANK, C), bf16),
            pltpu.VMEM((RANK, C), bf16),
            pltpu.VMEM((RANK, RANK), bf16),
            pltpu.VMEM((RANK, RANK), bf16),
        ],
        compiler_params=pltpu.CompilerParams(vmem_limit_bytes=50 << 20),
        name="outputs",
    )(momentum, grad, p, inv, rt, scale)


def body(momentum, grad, q_basis):
    p, inv, rt, scale = sums(momentum, grad, q_basis)
    return tuple(outputs(momentum, grad, p, inv, rt, scale))


def solution(mesh):
    return jax.shard_map(
        body,
        mesh=mesh,
        in_specs=(P("rows", "cols"), P("rows", "cols"), P("cols", None)),
        out_specs=(P("rows", "cols"), P("cols", None), P("rows", "cols")),
        check_vma=False,
    )
```

```python
import functools

import jax
import jax.numpy as jnp
from jax import lax
from jax.experimental import pallas as pl
from jax.experimental.pallas import tpu as pltpu
from jax.sharding import PartitionSpec as P

ROWS = 8192
COLS = 26624
RANK = 512
feedback_rate = 0.05
epsilon = 1e-05

R = 1024
C = 1664
B = 128
MESH = pl.DeviceIdType.MESH
f32 = jnp.float32
bf16 = jnp.bfloat16
NN = (((1,), (0,)), ((), ()))
NT = (((1,), (1,)), ((), ()))


def mm(a, b, dims):
    return lax.dot_general(a, b, dims, preferred_element_type=f32)


def mm6(a, b, dims):
    return lax.dot_general(a, b, dims, precision=lax.Precision.HIGHEST, preferred_element_type=f32)


def split(a):
    hi = a.astype(bf16)
    return hi, (a - hi.astype(f32)).astype(bf16)


def mm3(a, b, dims):
    return mm(a[0], b[0], dims) + (mm(a[0], b[1], dims) + mm(a[1], b[0], dims))


def tree(terms):
    while len(terms) > 1:
        terms = [a + b for a, b in zip(terms[::2], terms[1::2])]
    return terms[0]


def inverse_factor(block):
    lane = lax.broadcasted_iota(jnp.int32, (8, B), 1)
    sub = lax.broadcasted_iota(jnp.int32, (8, B), 0)
    rows = [block[8 * v : 8 * v + 8, :] for v in range(16)]

    def row(x, l):
        return jnp.broadcast_to(x[l : l + 1, :], (8, B))

    def column(x, l):
        return jnp.broadcast_to(x[:, l : l + 1], (8, B))

    out = []
    for g in range(16):
        o = 8 * g
        active = (lane >= o) & (lane < o + 8)
        c = [column(rows[g], o + m) for m in range(8)]
        e = jnp.where(active, jnp.where(lane - o == sub, 1.0, 0.0), rows[g])
        e_row = [row(e, m) for m in range(8)]
        low = [jnp.where(sub == m, 1.0, 0.0) for m in range(8)]
        pivots = jnp.ones((8, B), f32)
        for l in range(8):
            here = sub == l
            r = [row(c[m], l) for m in range(8)]
            inverse = 1.0 / r[l]
            pivots = jnp.where(here, c[l], pivots)
            for m in range(l):
                low[m] = jnp.where(here, c[m], low[m])
            factor = jnp.where(here, -1.0, c[l])
            for m in range(8):
                if m != l:
                    c[m] = jnp.where(here, 0.0, c[m]) - (factor * r[m]) * inverse
            c[l] = -(factor * inverse)
        t = tree([low[m] * e_row[m] for m in range(8)])
        out.append(lax.rsqrt(pivots) * jnp.where(lane < o + 8, t, 0.0))
        if g == 15:
            break
        w = tree([c[m] * e_row[m] for m in range(8)])
        w_row = [row(w, m) for m in range(8)]
        for v in range(g + 1, 16):
            step = tree([column(rows[v], o + m) * w_row[m] for m in range(8)])
            rows[v] = jnp.where(active, 0.0, rows[v]) - step
    return jnp.concatenate(out, axis=0)


def factor_step(k, gram, inv):
    o, p = B * k, B * (k + 1)
    diagonal = inverse_factor(gram[o:p, o:p])
    if k > 0:
        inv[o:p, 0:o] = mm6(diagonal, inv[o:p, 0:o], NN)
    inv[o:p, o:p] = diagonal
    if k < 3:
        low = mm6(gram[p:, o:p], diagonal, NT)
        gram[p:, p:] = gram[p:, p:] - mm6(low, low, NT)
        inv[p:, 0:p] = inv[p:, 0:p] - mm6(low, inv[o:p, 0:p], NN)


PACKED = [(0, 0), (1, 0), (1, 1), (2, 0), (2, 1), (2, 2), (3, 0), (3, 1), (3, 2), (3, 3)]
LANES = [(256 * j, min(256, C - 256 * j)) for j in range(7)]
N_MSG = 78


def sum_kernel(
    mom_hbm, grad_hbm, q_ref,
    orth_hbm, r_hi_hbm, r_lo_hbm, right_hbm, scale_ref,
    mom, grad, hi, lo, part, recv1, mid, recv2, p_buf, pt_hi, pt_lo,
    packed, g_recv0, g_recv1, g_sum, gram, inv, wt, w_recv0, w_recv1, w_sum,
    orth, r_hi, r_lo, right, col, col_recv,
    load_sem, save_sem, send_sem, recv_sem,
):
    row, column = lax.axis_index("rows"), lax.axis_index("cols")
    x, core = row // 2, row % 2
    y, z = column // 4, column % 4

    def at_x(d):
        return (((x + d) % 4) * 2 + core, column)

    def at_y(d):
        return (row, ((y + d) % 4) * 4 + z)

    def at_z(d):
        return (row, y * 4 + (z + d) % 4)

    other_core = (x * 2 + 1 - core, column)

    def block(start, size):
        return pl.ds(pl.multiple_of(start, size), size)

    loads = []
    for i in range(4):
        rows = pl.ds(256 * i, 256)
        pair = [
            pltpu.make_async_copy(mom_hbm.at[rows], mom.at[rows], load_sem.at[2 * i]),
            pltpu.make_async_copy(grad_hbm.at[rows], grad.at[rows], load_sem.at[2 * i + 1]),
        ]
        for copy in pair:
            copy.start()
        loads.append(pair)

    barrier = pltpu.get_barrier_semaphore()
    peers = [f(d) for f in (at_x, at_y, at_z) for d in (1, 2, 3)] + [other_core]
    for peer in peers:
        pl.semaphore_signal(barrier, inc=1, device_id=peer, device_id_type=MESH)
    pl.semaphore_wait(barrier, len(peers))

    started = []

    def send(src, dst, peer):
        number = len(started)
        copy = pltpu.make_async_remote_copy(
            src_ref=src, dst_ref=dst, send_sem=send_sem.at[number], recv_sem=recv_sem.at[number],
            device_id=peer, device_id_type=MESH,
        )
        copy.start()
        started.append(copy)
        return copy

    def finish(copies):
        for copy in copies:
            copy.wait_recv()

    at_first, at_second = (at_y, at_z), (at_z, at_y)
    first, second = (y, z), (z, y)
    groups = lambda s: [(2 * s + h, h) for h in range(2)]

    def product_p(s, i):
        rows = pl.ds(256 * i, 256)
        q = q_ref[:, 256 * s : 256 * s + 256]
        value = mm(hi[rows, :], q, NN) + mm(lo[rows, :], q, NN)
        part[2 * s, rows, :] = value[:, :B]
        part[2 * s + 1, rows, :] = value[:, B:]

    def scatter_first(s):
        copies = []
        for d in (2, 1, 3):
            for k, h in groups(s):
                rows = block(((first[h] + d) % 4) * 256, 256)
                copies.append(send(part.at[k, rows], recv1.at[k, d - 1], at_first[h](d)))
        return copies

    def scatter_second(s):
        copies = []
        for k, h in groups(s):
            rows = block(first[h] * 256, 256)
            mid[k] = (part[k, rows, :] + recv1[k, 0]) + (recv1[k, 1] + recv1[k, 2])
            for d in (2, 1, 3):
                rows = block(((second[h] + d) % 4) * 64, 64)
                copies.append(send(mid.at[k, rows], recv2.at[k, d - 1], at_second[h](d)))
        return copies

    def gather_second(s):
        copies = []
        for k, h in groups(s):
            rows = block(second[h] * 64, 64)
            mine = block(first[h] * 256 + second[h] * 64, 64)
            p_buf[k, mine, :] = (mid[k, rows, :] + recv2[k, 0]) + (recv2[k, 1] + recv2[k, 2])
            for d in (2, 1, 3):
                copies.append(send(p_buf.at[k, mine], p_buf.at[k, mine], at_second[h](d)))
        return copies

    def gather_first(s):
        copies = []
        for k, h in groups(s):
            mine = block(first[h] * 256, 256)
            for d in (2, 1, 3):
                copies.append(send(p_buf.at[k, mine], p_buf.at[k, mine], at_first[h](d)))
        return copies

    for i in range(4):
        for copy in loads[i]:
            copy.wait()

        @pl.loop(0, 8)
        def _(j):
            rows = block(256 * i + 32 * j, 32)
            top, rest = split(mom[rows, :] + grad[rows, :].astype(f32))
            hi[rows, :] = top
            lo[rows, :] = rest

        product_p(0, i)
    p1_0 = scatter_first(0)
    for i in range(4):
        product_p(1, i)
    p1_1 = scatter_first(1)
    finish(p1_0)
    p2_0 = scatter_second(0)
    finish(p1_1)
    p2_1 = scatter_second(1)
    finish(p2_0)
    p3_0 = gather_second(0)
    finish(p2_1)
    p3_1 = gather_second(1)
    finish(p3_0)
    p4_0 = gather_first(0)
    finish(p3_1)
    p4_1 = gather_first(1)

    def transpose_p(s):
        for k, _ in groups(s):
            for i in range(4):
                rows = slice(256 * i, 256 * i + 256)
                top, rest = split(p_buf[k, rows, :].T)
                pt_hi[B * k : B * k + B, rows] = top
                pt_lo[B * k : B * k + B, rows] = rest

    def gram_block(s, t):
        a, b = slice(256 * s, 256 * s + 256), slice(256 * t, 256 * t + 256)
        value = mm(pt_lo[a, :], pt_lo[b, :], NT) + mm3((pt_hi[a, :], pt_lo[a, :]), (pt_hi[b, :], pt_lo[b, :]), NT)
        for n, (i, j) in enumerate(PACKED):
            if i // 2 == s and j // 2 == t:
                r, c = B * (i % 2), B * (j % 2)
                packed[B * n : B * n + B, :] = value[r : r + B, c : c + B]

    def product_w(s):
        rows = slice(256 * s, 256 * s + 256)

        def chunk(lanes):
            wt[rows, lanes] = mm3((pt_hi[rows, :], pt_lo[rows, :]), (hi[:, lanes], lo[:, lanes]), NN)

        @pl.loop(0, 6)
        def _(j):
            chunk(block(256 * j, 256))

        chunk(slice(1536, 1664))

    def ours(s):
        return block(256 * s + B * core, B)

    def theirs(s):
        return block(256 * s + B * (1 - core), B)

    def slab(s, i):
        return block(256 * s + B * core + 32 * i, 32)

    def w_cores(s):
        return [send(wt.at[theirs(s)], w_recv0.at[s], other_core)]

    def w_scatter(s):
        wt[ours(s), :] = wt[ours(s), :] + w_recv0[s]
        return [send(wt.at[slab(s, (x + d) % 4)], w_recv1.at[s, d - 1], at_x(d)) for d in (2, 1, 3)]

    def w_gather(s):
        mine = slab(s, x)
        w_sum[mine, :] = (wt[mine, :] + w_recv1[s, 0]) + (w_recv1[s, 1] + w_recv1[s, 2])
        return [send(w_sum.at[mine], w_sum.at[mine], at_x(d)) for d in (2, 1, 3)]

    def w_back(s):
        return [send(w_sum.at[ours(s)], w_sum.at[ours(s)], other_core)]

    finish(p4_0)
    transpose_p(0)
    product_w(0)
    w0_0 = w_cores(0)
    gram_block(0, 0)
    finish(w0_0)
    w1_0 = w_scatter(0)
    finish(p4_1)
    transpose_p(1)
    gram_block(1, 0)
    gram_block(1, 1)
    g_ours, g_theirs = block(640 * core, 640), block(640 * (1 - core), 640)
    g0 = [send(packed.at[g_theirs], g_recv0, other_core)]
    product_w(1)
    w0_1 = w_cores(1)
    finish(g0)
    packed[g_ours, :] = packed[g_ours, :] + g_recv0[...]

    def g_slab(i):
        return block(640 * core + 160 * i, 160)

    g1 = [send(packed.at[g_slab((x + d) % 4)], g_recv1.at[d - 1], at_x(d)) for d in (2, 1, 3)]
    finish(w0_1)
    finish(g1)
    g_mine = g_slab(x)
    g_sum[g_mine, :] = (packed[g_mine, :] + g_recv1[0]) + (g_recv1[1] + g_recv1[2])
    g2 = [send(g_sum.at[g_mine], g_sum.at[g_mine], at_x(d)) for d in (2, 1, 3)]
    w1_1 = w_scatter(1)
    finish(w1_0)
    w2_0 = w_gather(0)
    finish(g2)
    g3 = [send(g_sum.at[g_ours], g_sum.at[g_ours], other_core)]
    inv[...] = jnp.zeros((RANK, RANK), f32)
    finish(g3)
    for n, (i, j) in enumerate(PACKED):
        gram[B * i : B * i + B, B * j : B * j + B] = g_sum[B * n : B * n + B, :]

    factor_step(0, gram, inv)
    finish(w1_1)
    w2_1 = w_gather(1)
    factor_step(1, gram, inv)
    factor_step(2, gram, inv)
    finish(w2_0)
    w3_0 = w_back(0)
    factor_step(3, gram, inv)
    finish(w2_1)
    w3_1 = w_back(1)
    finish(w3_0 + w3_1)

    inv_hi, inv_lo = split(inv[...])
    squares = jnp.zeros((RANK, B), f32)
    for start, size in LANES:
        lanes = slice(start, start + size)
        w = split(w_sum[:, lanes])
        top = mm3((inv_hi[:256, :256], inv_lo[:256, :256]), (w[0][:256], w[1][:256]), NN)
        bottom = mm3((inv_hi[256:], inv_lo[256:]), w, NN)
        r = jnp.concatenate([top, bottom], axis=0)
        mom[0:RANK, lanes] = r
        r_hi[:, lanes], r_lo[:, lanes] = split(r)
        for i in range(0, size, B):
            squares = squares + r[:, i : i + B] * r[:, i : i + B]
    saves = []

    def save(src, dst):
        copy = pltpu.make_async_copy(src, dst, save_sem.at[len(saves)])
        copy.start()
        saves.append(copy)

    save(r_hi, r_hi_hbm)
    save(r_lo, r_lo_hbm)
    col[0] = mm6(jnp.ones((8, B), f32), squares, NT)
    s1 = [send(col.at[0], col_recv.at[0, d - 1], at_y(d)) for d in (2, 1, 3)]
    for i in range(4):
        rows = slice(256 * i, 256 * i + 256)
        p = split(jnp.concatenate([p_buf[k, rows, :] for k in range(4)], axis=1))
        orth[rows, :] = mm3(p, (inv_hi, inv_lo), NT)
    save(orth, orth_hbm)
    finish(s1)
    col[1] = (col[0] + col_recv[0, 0]) + (col_recv[0, 1] + col_recv[0, 2])
    s2 = [send(col.at[1], col_recv.at[1, d - 1], at_z(d)) for d in (2, 1, 3)]
    for j in range(13):
        lanes = slice(B * j, B * j + B)
        right[lanes, :] = mom[0:RANK, lanes].T
    save(right, right_hbm)
    finish(s2)
    total = (col[1] + col_recv[1, 0]) + (col_recv[1, 1] + col_recv[1, 2])
    scale_ref[...] = lax.rsqrt(total * (1.0 / COLS) + epsilon)
    for copy in saves:
        copy.wait()
    for copy in started:
        copy.wait_send()


def sums(momentum, grad, q_basis):
    vmem = pl.BlockSpec(memory_space=pltpu.VMEM)
    hbm = pl.BlockSpec(memory_space=pl.ANY)
    return pl.pallas_call(
        sum_kernel,
        out_shape=[
            jax.ShapeDtypeStruct((R, RANK), f32),
            jax.ShapeDtypeStruct((RANK, C), bf16),
            jax.ShapeDtypeStruct((RANK, C), bf16),
            jax.ShapeDtypeStruct((C, RANK), f32),
            jax.ShapeDtypeStruct((8, RANK), f32),
        ],
        in_specs=[hbm, hbm, vmem],
        out_specs=[hbm] * 4 + [vmem],
        scratch_shapes=[
            pltpu.VMEM((R, C), f32),
            pltpu.VMEM((R, C), bf16),
            pltpu.VMEM((R, C), bf16),
            pltpu.VMEM((R, C), bf16),
            pltpu.VMEM((4, R, B), f32),
            pltpu.VMEM((4, 3, 256, B), f32),
            pltpu.VMEM((4, 256, B), f32),
            pltpu.VMEM((4, 3, 64, B), f32),
            pltpu.VMEM((4, R, B), f32),
            pltpu.VMEM((RANK, R), bf16),
            pltpu.VMEM((RANK, R), bf16),
            pltpu.VMEM((1280, B), f32),
            pltpu.VMEM((640, B), f32),
            pltpu.VMEM((3, 160, B), f32),
            pltpu.VMEM((1280, B), f32),
            pltpu.VMEM((RANK, RANK), f32),
            pltpu.VMEM((RANK, RANK), f32),
            pltpu.VMEM((RANK, C), f32),
            pltpu.VMEM((2, B, C), f32),
            pltpu.VMEM((2, 3, 32, C), f32),
            pltpu.VMEM((RANK, C), f32),
            pltpu.VMEM((R, RANK), f32),
            pltpu.VMEM((RANK, C), bf16),
            pltpu.VMEM((RANK, C), bf16),
            pltpu.VMEM((C, RANK), f32),
            pltpu.VMEM((2, 8, RANK), f32),
            pltpu.VMEM((2, 3, 8, RANK), f32),
            pltpu.SemaphoreType.DMA((8,)),
            pltpu.SemaphoreType.DMA((4,)),
            pltpu.SemaphoreType.DMA((N_MSG,)),
            pltpu.SemaphoreType.DMA((N_MSG,)),
        ],
        compiler_params=pltpu.CompilerParams(
            collective_id=0, has_side_effects=True, vmem_limit_bytes=60 << 20
        ),
        name="sums",
    )(momentum, grad, q_basis)


def output_kernel(mom, grad, orth_ref, r_hi, r_lo, right, scale_ref, mom_out, q_out, update_out):
    scale = scale_ref[0:1, :]
    q_out[...] = (right[...] * scale).astype(bf16)
    orth = orth_ref[...]
    scaled = split(orth * (scale * (float(ROWS) / RANK) ** 0.5))
    step = (orth * feedback_rate).astype(bf16)
    for start, size in LANES:
        lanes = slice(start, start + size)
        top = r_hi[:, lanes]
        merged = mom[:, lanes] + grad[:, lanes].astype(f32)
        mom_out[:, lanes] = merged - mm(step, top, NN)
        update_out[:, lanes] = mm3(scaled, (top, r_lo[:, lanes]), NN).astype(bf16)


def outputs(momentum, grad, orth, r_hi, r_lo, right, scale):
    steps = 4
    rows = R // steps
    whole = lambda *shape: pl.BlockSpec(shape, lambda i: (0,) * len(shape))
    slab = lambda n, width: pl.BlockSpec((n // steps, width), lambda i: (i, 0))
    return pl.pallas_call(
        output_kernel,
        grid=(steps,),
        out_shape=[
            jax.ShapeDtypeStruct((R, C), f32),
            jax.ShapeDtypeStruct((C, RANK), bf16),
            jax.ShapeDtypeStruct((R, C), bf16),
        ],
        in_specs=[
            slab(R, C), slab(R, C), slab(R, RANK), whole(RANK, C), whole(RANK, C), slab(C, RANK), whole(8, RANK),
        ],
        out_specs=[slab(R, C), slab(C, RANK), slab(R, C)],
        compiler_params=pltpu.CompilerParams(vmem_limit_bytes=60 << 20),
        name="outputs",
    )(momentum, grad, orth, r_hi, r_lo, right, scale)


def body(momentum, grad, q_basis):
    return tuple(outputs(momentum, grad, *sums(momentum, grad, q_basis)))


def solution(mesh):
    return jax.shard_map(
        body,
        mesh=mesh,
        in_specs=(P("rows", "cols"), P("rows", "cols"), P("cols", None)),
        out_specs=(P("rows", "cols"), P("cols", None), P("rows", "cols")),
        check_vma=False,
    )
```

```python
import functools

import jax
import jax.numpy as jnp
from jax import lax
from jax.experimental import pallas as pl
from jax.experimental.pallas import tpu as pltpu
from jax.sharding import PartitionSpec as P

ROWS = 8192
COLS = 26624
RANK = 512
feedback_rate = 0.05
epsilon = 1e-05

R = 1024
C = 1664
B = 128
MESH = pl.DeviceIdType.MESH
f32 = jnp.float32
bf16 = jnp.bfloat16
NN = (((1,), (0,)), ((), ()))
NT = (((1,), (1,)), ((), ()))


def mm(a, b, dims):
    return lax.dot_general(a, b, dims, preferred_element_type=f32)


def mm6(a, b, dims):
    return lax.dot_general(a, b, dims, precision=lax.Precision.HIGHEST, preferred_element_type=f32)


def split(a):
    hi = a.astype(bf16)
    return hi, (a - hi.astype(f32)).astype(bf16)


def mm3(a, b, dims):
    return mm(a[0], b[0], dims) + (mm(a[0], b[1], dims) + mm(a[1], b[0], dims))


def tree(terms):
    while len(terms) > 1:
        terms = [a + b for a, b in zip(terms[::2], terms[1::2])]
    return terms[0]


def inverse_factor(block):
    lane = lax.broadcasted_iota(jnp.int32, (8, B), 1)
    sub = lax.broadcasted_iota(jnp.int32, (8, B), 0)
    rows = [block[8 * v : 8 * v + 8, :] for v in range(16)]

    def row(x, l):
        return jnp.broadcast_to(x[l : l + 1, :], (8, B))

    def column(x, l):
        return jnp.broadcast_to(x[:, l : l + 1], (8, B))

    out = []
    for g in range(16):
        o = 8 * g
        active = (lane >= o) & (lane < o + 8)
        c = [column(rows[g], o + m) for m in range(8)]
        e = jnp.where(active, jnp.where(lane - o == sub, 1.0, 0.0), rows[g])
        e_row = [row(e, m) for m in range(8)]
        low = [jnp.where(sub == m, 1.0, 0.0) for m in range(8)]
        pivots = jnp.ones((8, B), f32)
        for l in range(0, 8, 2):
            at0, at1 = sub == l, sub == l + 1
            r = [row(c[m], l) for m in range(8)]
            s = [row(c[m], l + 1) for m in range(8)]
            p, q, t = r[l], r[l + 1], s[l + 1]
            inverse = 1.0 / (p * t - q * q)
            ratio = q / p
            pivots = jnp.where(at0, p, jnp.where(at1, t - ratio * q, pivots))
            for m in range(l):
                low[m] = jnp.where(at0, r[m], jnp.where(at1, s[m] - ratio * r[m], low[m]))
            low[l] = jnp.where(at1, -ratio, low[l])
            u = jnp.where(at0, -t, jnp.where(at1, q, t * c[l] - q * c[l + 1]))
            v = jnp.where(at0, q, jnp.where(at1, -p, p * c[l + 1] - q * c[l]))
            for m in range(8):
                if m not in (l, l + 1):
                    c[m] = jnp.where(at0 | at1, 0.0, c[m]) - (r[m] * u + s[m] * v) * inverse
            c[l], c[l + 1] = -(u * inverse), -(v * inverse)
        t = tree([low[m] * e_row[m] for m in range(8)])
        out.append(lax.rsqrt(pivots) * jnp.where(lane < o + 8, t, 0.0))
        if g == 15:
            break
        w = tree([c[m] * e_row[m] for m in range(8)])
        w_row = [row(w, m) for m in range(8)]
        for v in range(g + 1, 16):
            step = tree([column(rows[v], o + m) * w_row[m] for m in range(8)])
            rows[v] = jnp.where(active, 0.0, rows[v]) - step
    return jnp.concatenate(out, axis=0)


def factor_step(k, diagonal, gram, inv):
    o, p, n = B * k, B * (k + 1), B * (k + 2)
    x = inverse_factor(diagonal)
    inv[o:p, o:p] = x
    if k < 3:
        near = mm6(gram[p:n, o:p], x, NT)
        diagonal = gram[p:n, p:n] - mm6(near, near, NT)
    if k > 0:
        inv[o:p, 0:o] = mm6(x, inv[o:p, 0:o], NN)
    if k < 3:
        low = near
        if k < 2:
            far = mm6(gram[n:, o:p], x, NT)
            gram[n:, p:n] = gram[n:, p:n] - mm6(far, near, NT)
            gram[n:, n:] = gram[n:, n:] - mm6(far, far, NT)
            low = jnp.concatenate([near, far], axis=0)
        inv[p:, 0:p] = inv[p:, 0:p] - mm6(low, inv[o:p, 0:p], NN)
    return diagonal


PACKED = [(0, 0), (1, 0), (1, 1), (2, 0), (2, 1), (2, 2), (3, 0), (3, 1), (3, 2), (3, 3)]
LANES = [(256 * j, min(256, C - 256 * j)) for j in range(7)]
N_MSG = 87


def sum_kernel(
    mom_hbm, grad_hbm, q_ref,
    orth_hbm, r_hi_hbm, r_lo_hbm, scale_ref,
    mom, grad, hi, lo, part, recv1, mid, recv2, p_buf, pt_hi, pt_lo,
    packed, g_recv0, g_recv1, g_sum, gram, inv, w_recv0, w_recv1,
    orth, col, col_recv,
    load_sem, save_sem, send_sem, recv_sem,
):
    wt, w_sum = mom.at[0:RANK], mom.at[RANK:R]
    r_hi, r_lo = grad.at[0:RANK], grad.at[RANK:R]
    row, column = lax.axis_index("rows"), lax.axis_index("cols")
    x, core = row // 2, row % 2
    y, z = column // 4, column % 4

    def at_x(d):
        return (((x + d) % 4) * 2 + core, column)

    def at_y(d):
        return (row, ((y + d) % 4) * 4 + z)

    def at_z(d):
        return (row, y * 4 + (z + d) % 4)

    other_core = (x * 2 + 1 - core, column)

    def block(start, size):
        return pl.ds(pl.multiple_of(start, size), size)

    loads = []
    for i in range(4):
        rows = pl.ds(256 * i, 256)
        pair = [
            pltpu.make_async_copy(mom_hbm.at[rows], mom.at[rows], load_sem.at[2 * i]),
            pltpu.make_async_copy(grad_hbm.at[rows], grad.at[rows], load_sem.at[2 * i + 1]),
        ]
        for copy in pair:
            copy.start()
        loads.append(pair)

    barrier = pltpu.get_barrier_semaphore()

    def at_plane(d):
        return (row, (column + d) % 16)

    peers = [at_x(d) for d in (1, 2, 3)] + [at_plane(d) for d in range(1, 16)] + [other_core]
    for peer in peers:
        pl.semaphore_signal(barrier, inc=1, device_id=peer, device_id_type=MESH)

    started = []

    def send(src, dst, peer):
        number = len(started)
        copy = pltpu.make_async_remote_copy(
            src_ref=src, dst_ref=dst, send_sem=send_sem.at[number], recv_sem=recv_sem.at[number],
            device_id=peer, device_id_type=MESH,
        )
        copy.start()
        started.append(copy)
        return copy

    def finish(copies):
        for copy in copies:
            copy.wait_recv()

    at_first, at_second = (at_y, at_z), (at_z, at_y)
    first, second = (y, z), (z, y)
    groups = lambda s: [(2 * s + h, h) for h in range(2)]

    def product_p(s, i):
        rows = pl.ds(256 * i, 256)
        q = q_ref[:, 256 * s : 256 * s + 256]
        value = mm(hi[rows, :], q, NN) + mm(lo[rows, :], q, NN)
        part[2 * s, rows, :] = value[:, :B]
        part[2 * s + 1, rows, :] = value[:, B:]

    def scatter_first(s):
        copies = []
        for d in (2, 1, 3):
            for k, h in groups(s):
                rows = block(((first[h] + d) % 4) * 256, 256)
                copies.append(send(part.at[k, rows], recv1.at[k, d - 1], at_first[h](d)))
        return copies

    def scatter_second(s):
        copies = []
        for k, h in groups(s):
            rows = block(first[h] * 256, 256)
            mid[k] = (part[k, rows, :] + recv1[k, 0]) + (recv1[k, 1] + recv1[k, 2])
            for d in (2, 1, 3):
                rows = block(((second[h] + d) % 4) * 64, 64)
                copies.append(send(mid.at[k, rows], recv2.at[k, d - 1], at_second[h](d)))
        return copies

    def gather_second(s):
        copies = []
        for k, h in groups(s):
            rows = block(second[h] * 64, 64)
            mine = block(first[h] * 256 + second[h] * 64, 64)
            p_buf[k, mine, :] = (mid[k, rows, :] + recv2[k, 0]) + (recv2[k, 1] + recv2[k, 2])
            for d in (2, 1, 3):
                copies.append(send(p_buf.at[k, mine], p_buf.at[k, mine], at_second[h](d)))
        return copies

    def gather_first(s):
        copies = []
        for k, h in groups(s):
            mine = block(first[h] * 256, 256)
            for d in (2, 1, 3):
                copies.append(send(p_buf.at[k, mine], p_buf.at[k, mine], at_first[h](d)))
        return copies

    for i in range(4):
        for copy in loads[i]:
            copy.wait()

        @pl.loop(0, 8)
        def _(j):
            rows = block(256 * i + 32 * j, 32)
            top, rest = split(mom[rows, :] + grad[rows, :].astype(f32))
            hi[rows, :] = top
            lo[rows, :] = rest

        product_p(0, i)
    pl.semaphore_wait(barrier, len(peers))
    p1_0 = scatter_first(0)
    for i in range(4):
        product_p(1, i)
    finish(p1_0)
    p2_0 = scatter_second(0)
    p1_1 = scatter_first(1)
    finish(p2_0)
    p3_0 = gather_second(0)
    finish(p1_1)
    p2_1 = scatter_second(1)
    finish(p3_0)
    p4_0 = gather_first(0)
    finish(p2_1)
    p3_1 = gather_second(1)
    finish(p3_1)
    p4_1 = gather_first(1)

    def transpose_p(s):
        for k, _ in groups(s):
            for i in range(4):
                rows = slice(256 * i, 256 * i + 256)
                top, rest = split(p_buf[k, rows, :].T)
                pt_hi[B * k : B * k + B, rows] = top
                pt_lo[B * k : B * k + B, rows] = rest

    def gram_block(s, t):
        a, b = slice(256 * s, 256 * s + 256), slice(256 * t, 256 * t + 256)
        value = mm(pt_lo[a, :], pt_lo[b, :], NT) + mm3((pt_hi[a, :], pt_lo[a, :]), (pt_hi[b, :], pt_lo[b, :]), NT)
        for n, (i, j) in enumerate(PACKED):
            if i // 2 == s and j // 2 == t:
                r, c = B * (i % 2), B * (j % 2)
                packed[B * n : B * n + B, :] = value[r : r + B, c : c + B]

    def product_w(s):
        rows = slice(256 * s, 256 * s + 256)

        def chunk(lanes):
            wt[rows, lanes] = mm3((pt_hi[rows, :], pt_lo[rows, :]), (hi[:, lanes], lo[:, lanes]), NN)

        @pl.loop(0, 6)
        def _(j):
            chunk(block(256 * j, 256))

        chunk(slice(1536, 1664))

    def ours(s):
        return block(256 * s + B * core, B)

    def theirs(s):
        return block(256 * s + B * (1 - core), B)

    def slab(s, i):
        return block(256 * s + B * core + 32 * i, 32)

    def w_cores(s):
        return [send(wt.at[theirs(s)], w_recv0.at[s], other_core)]

    def w_scatter(s):
        wt[ours(s), :] = wt[ours(s), :] + w_recv0[s]
        return [send(wt.at[slab(s, (x + d) % 4)], w_recv1.at[s, d - 1], at_x(d)) for d in (2, 1, 3)]

    def w_gather(s):
        mine = slab(s, x)
        w_sum[mine, :] = (wt[mine, :] + w_recv1[s, 0]) + (w_recv1[s, 1] + w_recv1[s, 2])
        return [send(w_sum.at[mine], w_sum.at[mine], at_x(d)) for d in (2, 1, 3)]

    def w_back(s):
        return [send(w_sum.at[ours(s)], w_sum.at[ours(s)], other_core)]

    finish(p4_0)
    transpose_p(0)
    product_w(0)
    w0_0 = w_cores(0)
    gram_block(0, 0)
    finish(w0_0)
    w1_0 = w_scatter(0)
    finish(p4_1)
    transpose_p(1)
    gram_block(1, 0)
    gram_block(1, 1)
    g_ours, g_theirs = block(640 * core, 640), block(640 * (1 - core), 640)
    g0 = [send(packed.at[g_theirs], g_recv0, other_core)]
    product_w(1)
    w0_1 = w_cores(1)
    finish(g0)
    packed[g_ours, :] = packed[g_ours, :] + g_recv0[...]

    def g_slab(i):
        return block(640 * core + 160 * i, 160)

    g1 = [send(packed.at[g_slab((x + d) % 4)], g_recv1.at[d - 1], at_x(d)) for d in (2, 1, 3)]
    finish(w0_1)
    finish(g1)
    g_mine = g_slab(x)
    g_sum[g_mine, :] = (packed[g_mine, :] + g_recv1[0]) + (g_recv1[1] + g_recv1[2])
    g2 = [send(g_sum.at[g_mine], g_sum.at[g_mine], at_x(d)) for d in (2, 1, 3)]
    w1_1 = w_scatter(1)
    finish(w1_0)
    w2_0 = w_gather(0)
    finish(g2)
    g3 = [send(g_sum.at[g_ours], g_sum.at[g_ours], other_core)]
    inv[...] = jnp.zeros((RANK, RANK), f32)
    finish(g3)
    on = lax.broadcasted_iota(jnp.int32, (B, B), 0) == lax.broadcasted_iota(jnp.int32, (B, B), 1)
    diagonals = [jnp.where(on, g_sum[B * n : B * n + B, :], 0.0) for n in (0, 2, 5, 9)]
    down = [lax.rsqrt(jnp.sum(t, axis=1, keepdims=True)) for t in diagonals]
    across = [lax.rsqrt(jnp.sum(t, axis=0, keepdims=True)) for t in diagonals]
    for n, (i, j) in enumerate(PACKED):
        gram[B * i : B * i + B, B * j : B * j + B] = g_sum[B * n : B * n + B, :] * down[i] * across[j]

    diagonal = factor_step(0, gram[0:B, 0:B], gram, inv)
    finish(w1_1)
    w2_1 = w_gather(1)
    diagonal = factor_step(1, diagonal, gram, inv)
    finish(w2_0)
    w3_0 = w_back(0)
    diagonal = factor_step(2, diagonal, gram, inv)
    factor_step(3, diagonal, gram, inv)
    finish(w2_1)
    w3_1 = w_back(1)
    inv_hi, inv_lo = split(inv[...] * jnp.concatenate(across, axis=1))
    finish(w3_0 + w3_1)

    squares = jnp.zeros((RANK, B), f32)
    for start, size in LANES:
        lanes = slice(start, start + size)
        w = split(w_sum[:, lanes])
        top = mm3((inv_hi[:256, :256], inv_lo[:256, :256]), (w[0][:256], w[1][:256]), NN)
        bottom = mm3((inv_hi[256:], inv_lo[256:]), w, NN)
        r = jnp.concatenate([top, bottom], axis=0)
        r_hi[:, lanes], r_lo[:, lanes] = split(r)
        for i in range(0, size, B):
            squares = squares + r[:, i : i + B] * r[:, i : i + B]
    saves = []

    def save(src, dst):
        copy = pltpu.make_async_copy(src, dst, save_sem.at[len(saves)])
        copy.start()
        saves.append(copy)

    save(r_hi, r_hi_hbm)
    save(r_lo, r_lo_hbm)
    col[...] = mm6(jnp.ones((8, B), f32), squares, NT)
    exchange = [send(col, col_recv.at[d - 1], at_plane(d)) for d in range(1, 16)]
    for i in range(4):
        rows = slice(256 * i, 256 * i + 256)
        p = split(jnp.concatenate([p_buf[k, rows, :] for k in range(4)], axis=1))
        orth[rows, :] = mm3(p, (inv_hi, inv_lo), NT)
    save(orth, orth_hbm)
    finish(exchange)
    total = tree([col[...]] + [col_recv[d] for d in range(15)])
    scale_ref[...] = lax.rsqrt(total * (1.0 / COLS) + epsilon)
    for copy in saves:
        copy.wait()
    for copy in started:
        copy.wait_send()


def sums(momentum, grad, q_basis):
    vmem = pl.BlockSpec(memory_space=pltpu.VMEM)
    hbm = pl.BlockSpec(memory_space=pl.ANY)
    return pl.pallas_call(
        sum_kernel,
        out_shape=[
            jax.ShapeDtypeStruct((R, RANK), f32),
            jax.ShapeDtypeStruct((RANK, C), bf16),
            jax.ShapeDtypeStruct((RANK, C), bf16),
            jax.ShapeDtypeStruct((8, RANK), f32),
        ],
        in_specs=[hbm, hbm, vmem],
        out_specs=[hbm] * 3 + [vmem],
        scratch_shapes=[
            pltpu.VMEM((R, C), f32),
            pltpu.VMEM((R, C), bf16),
            pltpu.VMEM((R, C), bf16),
            pltpu.VMEM((R, C), bf16),
            pltpu.VMEM((4, R, B), f32),
            pltpu.VMEM((4, 3, 256, B), f32),
            pltpu.VMEM((4, 256, B), f32),
            pltpu.VMEM((4, 3, 64, B), f32),
            pltpu.VMEM((4, R, B), f32),
            pltpu.VMEM((RANK, R), bf16),
            pltpu.VMEM((RANK, R), bf16),
            pltpu.VMEM((1280, B), f32),
            pltpu.VMEM((640, B), f32),
            pltpu.VMEM((3, 160, B), f32),
            pltpu.VMEM((1280, B), f32),
            pltpu.VMEM((RANK, RANK), f32),
            pltpu.VMEM((RANK, RANK), f32),
            pltpu.VMEM((2, B, C), f32),
            pltpu.VMEM((2, 3, 32, C), f32),
            pltpu.VMEM((R, RANK), f32),
            pltpu.VMEM((8, RANK), f32),
            pltpu.VMEM((15, 8, RANK), f32),
            pltpu.SemaphoreType.DMA((8,)),
            pltpu.SemaphoreType.DMA((3,)),
            pltpu.SemaphoreType.DMA((N_MSG,)),
            pltpu.SemaphoreType.DMA((N_MSG,)),
        ],
        compiler_params=pltpu.CompilerParams(
            collective_id=0, has_side_effects=True, vmem_limit_bytes=44 << 20
        ),
        name="sums",
    )(momentum, grad, q_basis)


STEPS = 4
Q_CHUNKS = [range(13 * i // STEPS, 13 * (i + 1) // STEPS) for i in range(STEPS)]


def output_kernel(mom, grad, orth_ref, r_hi, r_lo, scale_ref, mom_out, q_out, update_out):
    scale = scale_ref[0:1, :]
    for i, chunks in enumerate(Q_CHUNKS):

        @pl.when(pl.program_id(0) == i)
        def _(chunks=chunks):
            for j in chunks:
                lanes = slice(B * j, B * j + B)
                r = r_hi[:, lanes].astype(f32) + r_lo[:, lanes].astype(f32)
                q_out[lanes, :] = (r.T * scale).astype(bf16)

    orth = orth_ref[...]
    scaled = split(orth * (scale * (float(ROWS) / RANK) ** 0.5))
    step = (orth * feedback_rate).astype(bf16)
    for start, size in LANES:
        lanes = slice(start, start + size)
        top = r_hi[:, lanes]
        merged = mom[:, lanes] + grad[:, lanes].astype(f32)
        mom_out[:, lanes] = merged - mm(step, top, NN)
        update_out[:, lanes] = mm3(scaled, (top, r_lo[:, lanes]), NN).astype(bf16)


def outputs(momentum, grad, orth, r_hi, r_lo, scale):
    whole = lambda *shape: pl.BlockSpec(shape, lambda i: (0,) * len(shape))
    slab = lambda width: pl.BlockSpec((R // STEPS, width), lambda i: (i, 0))
    return pl.pallas_call(
        output_kernel,
        grid=(STEPS,),
        out_shape=[
            jax.ShapeDtypeStruct((R, C), f32),
            jax.ShapeDtypeStruct((C, RANK), bf16),
            jax.ShapeDtypeStruct((R, C), bf16),
        ],
        in_specs=[slab(C), slab(C), slab(RANK), whole(RANK, C), whole(RANK, C), whole(8, RANK)],
        out_specs=[slab(C), whole(C, RANK), slab(C)],
        compiler_params=pltpu.CompilerParams(vmem_limit_bytes=36 << 20),
        name="outputs",
    )(momentum, grad, orth, r_hi, r_lo, scale)


def body(momentum, grad, q_basis):
    return tuple(outputs(momentum, grad, *sums(momentum, grad, q_basis)))


def solution(mesh):
    return jax.shard_map(
        body,
        mesh=mesh,
        in_specs=(P("rows", "cols"), P("rows", "cols"), P("cols", None)),
        out_specs=(P("rows", "cols"), P("cols", None), P("rows", "cols")),
        check_vma=False,
    )
```

```python
import functools

import jax
import jax.numpy as jnp
from jax import lax
from jax.experimental import pallas as pl
from jax.experimental.pallas import tpu as pltpu
from jax.sharding import PartitionSpec as P

ROWS = 8192
COLS = 26624
RANK = 512
feedback_rate = 0.05
epsilon = 1e-05

R = 1024
C = 1664
B = 128
MESH = pl.DeviceIdType.MESH
f32 = jnp.float32
bf16 = jnp.bfloat16
NN = (((1,), (0,)), ((), ()))
NT = (((1,), (1,)), ((), ()))


def mm(a, b, dims):
    return lax.dot_general(a, b, dims, preferred_element_type=f32)


def mm6(a, b, dims):
    return lax.dot_general(a, b, dims, precision=lax.Precision.HIGHEST, preferred_element_type=f32)


def split(a):
    hi = a.astype(bf16)
    return hi, (a - hi.astype(f32)).astype(bf16)


def mm3(a, b, dims):
    return mm(a[0], b[0], dims) + (mm(a[0], b[1], dims) + mm(a[1], b[0], dims))


def tree(terms):
    while len(terms) > 1:
        terms = [a + b for a, b in zip(terms[::2], terms[1::2])]
    return terms[0]


def inverse_factor(block):
    lane = lax.broadcasted_iota(jnp.int32, (8, B), 1)
    sub = lax.broadcasted_iota(jnp.int32, (8, B), 0)
    rows = [block[8 * v : 8 * v + 8, :] for v in range(16)]

    def row(x, l):
        return jnp.broadcast_to(x[l : l + 1, :], (8, B))

    def column(x, l):
        return jnp.broadcast_to(x[:, l : l + 1], (8, B))

    out = []
    for g in range(16):
        o = 8 * g
        active = (lane >= o) & (lane < o + 8)
        c = [column(rows[g], o + m) for m in range(8)]
        e = jnp.where(active, jnp.where(lane - o == sub, 1.0, 0.0), rows[g])
        e_row = [row(e, m) for m in range(8)]
        low = [jnp.where(sub == m, 1.0, 0.0) for m in range(8)]
        pivots = jnp.ones((8, B), f32)
        for l in range(0, 8, 2):
            at0, at1 = sub == l, sub == l + 1
            r = [row(c[m], l) for m in range(8)]
            s = [row(c[m], l + 1) for m in range(8)]
            p, q, t = r[l], r[l + 1], s[l + 1]
            inverse = 1.0 / (p * t - q * q)
            ratio = q / p
            pivots = jnp.where(at0, p, jnp.where(at1, t - ratio * q, pivots))
            for m in range(l):
                low[m] = jnp.where(at0, r[m], jnp.where(at1, s[m] - ratio * r[m], low[m]))
            low[l] = jnp.where(at1, -ratio, low[l])
            u = jnp.where(at0, -t, jnp.where(at1, q, t * c[l] - q * c[l + 1]))
            v = jnp.where(at0, q, jnp.where(at1, -p, p * c[l + 1] - q * c[l]))
            for m in range(8):
                if m not in (l, l + 1):
                    c[m] = jnp.where(at0 | at1, 0.0, c[m]) - (r[m] * u + s[m] * v) * inverse
            c[l], c[l + 1] = -(u * inverse), -(v * inverse)
        t = tree([low[m] * e_row[m] for m in range(8)])
        out.append(lax.rsqrt(pivots) * jnp.where(lane < o + 8, t, 0.0))
        if g == 15:
            break
        w = tree([c[m] * e_row[m] for m in range(8)])
        w_row = [row(w, m) for m in range(8)]
        for v in range(g + 1, 16):
            step = tree([column(rows[v], o + m) * w_row[m] for m in range(8)])
            rows[v] = jnp.where(active, 0.0, rows[v]) - step
    return jnp.concatenate(out, axis=0)


def factor_step(k, diagonal, gram, inv):
    o, p, n = B * k, B * (k + 1), B * (k + 2)
    x = inverse_factor(diagonal)
    inv[o:p, o:p] = x
    if k < 3:
        near = mm6(gram[p:n, o:p], x, NT)
        diagonal = gram[p:n, p:n] - mm6(near, near, NT)
    if k > 0:
        inv[o:p, 0:o] = mm6(x, inv[o:p, 0:o], NN)
    if k < 3:
        low = near
        if k < 2:
            far = mm6(gram[n:, o:p], x, NT)
            gram[n:, p:n] = gram[n:, p:n] - mm6(far, near, NT)
            gram[n:, n:] = gram[n:, n:] - mm6(far, far, NT)
            low = jnp.concatenate([near, far], axis=0)
        inv[p:, 0:p] = inv[p:, 0:p] - mm6(low, inv[o:p, 0:p], NN)
    return diagonal


PACKED = [(0, 0), (1, 0), (1, 1), (2, 0), (2, 1), (2, 2), (3, 0), (3, 1), (3, 2), (3, 3)]
LANES = [(256 * j, min(256, C - 256 * j)) for j in range(7)]
N_MSG = 91


def sum_kernel(
    mom_hbm, grad_hbm, q_hbm,
    orth_hbm, r_hi_hbm, r_lo_hbm, scale_ref,
    mom, grad, q_ref, hi, lo, part, recv1, mid, recv2, p_buf, pt_hi, pt_lo,
    packed, g_recv0, g_recv1, g_sum, gram, inv, w_recv0, w_recv1, w_recv2,
    orth, col, col_recv,
    load_sem, save_sem, send_sem, recv_sem,
):
    wt, w_sum = mom.at[0:RANK], mom.at[RANK:R]
    r_hi, r_lo = grad.at[0:RANK], grad.at[RANK:R]
    row, column = lax.axis_index("rows"), lax.axis_index("cols")
    x, core = row // 2, row % 2
    y, z = column // 4, column % 4

    def at_x(d):
        return (((x + d) % 4) * 2 + core, column)

    def at_y(d):
        return (row, ((y + d) % 4) * 4 + z)

    def at_z(d):
        return (row, y * 4 + (z + d) % 4)

    other_core = (x * 2 + 1 - core, column)

    def block(start, size):
        return pl.ds(pl.multiple_of(start, size), size)

    loads = []
    for i in range(4):
        rows = pl.ds(256 * i, 256)
        pair = [
            pltpu.make_async_copy(mom_hbm.at[rows], mom.at[rows], load_sem.at[2 * i]),
            pltpu.make_async_copy(grad_hbm.at[rows], grad.at[rows], load_sem.at[2 * i + 1]),
        ]
        for copy in pair:
            copy.start()
        loads.append(pair)
        if i == 0:
            load_q = pltpu.make_async_copy(q_hbm, q_ref, load_sem.at[8])
            load_q.start()

    barrier = pltpu.get_barrier_semaphore()

    def at_plane(d):
        return (row, (column + d) % 16)

    peers = [at_x(d) for d in (1, 2, 3)] + [at_plane(d) for d in range(1, 16)] + [other_core]
    for peer in peers:
        pl.semaphore_signal(barrier, inc=1, device_id=peer, device_id_type=MESH)

    started = []

    def send(src, dst, peer):
        number = len(started)
        copy = pltpu.make_async_remote_copy(
            src_ref=src, dst_ref=dst, send_sem=send_sem.at[number], recv_sem=recv_sem.at[number],
            device_id=peer, device_id_type=MESH,
        )
        copy.start()
        started.append(copy)
        return copy

    def finish(copies):
        for copy in copies:
            copy.wait_recv()

    at_first, at_second = (at_y, at_z), (at_z, at_y)
    first, second = (y, z), (z, y)
    groups = lambda s: [(2 * s + h, h) for h in range(2)]

    def product_p(s, i):
        rows = pl.ds(256 * i, 256)
        q = q_ref[:, 256 * s : 256 * s + 256]
        value = mm(hi[rows, :], q, NN) + mm(lo[rows, :], q, NN)
        part[2 * s, rows, :] = value[:, :B]
        part[2 * s + 1, rows, :] = value[:, B:]

    def scatter_first(s):
        copies = []
        for d in (2, 1, 3):
            for k, h in groups(s):
                rows = block(((first[h] + d) % 4) * 256, 256)
                copies.append(send(part.at[k, rows], recv1.at[k, d - 1], at_first[h](d)))
        return copies

    def scatter_second(s):
        copies = []
        for k, h in groups(s):
            rows = block(first[h] * 256, 256)
            mid[k] = (part[k, rows, :] + recv1[k, 0]) + (recv1[k, 1] + recv1[k, 2])
            for d in (2, 1, 3):
                rows = block(((second[h] + d) % 4) * 64, 64)
                copies.append(send(mid.at[k, rows], recv2.at[k, d - 1], at_second[h](d)))
        return copies

    def gather_second(s):
        copies = []
        for k, h in groups(s):
            rows = block(second[h] * 64, 64)
            mine = block(first[h] * 256 + second[h] * 64, 64)
            p_buf[k, mine, :] = (mid[k, rows, :] + recv2[k, 0]) + (recv2[k, 1] + recv2[k, 2])
            for d in (2, 1, 3):
                copies.append(send(p_buf.at[k, mine], p_buf.at[k, mine], at_second[h](d)))
        return copies

    def gather_first(s):
        copies = []
        for k, h in groups(s):
            mine = block(first[h] * 256, 256)
            for d in (2, 1, 3):
                copies.append(send(p_buf.at[k, mine], p_buf.at[k, mine], at_first[h](d)))
        return copies

    for i in range(4):
        for copy in loads[i]:
            copy.wait()

        @pl.loop(0, 8)
        def _(j):
            rows = block(256 * i + 32 * j, 32)
            top, rest = split(mom[rows, :] + grad[rows, :].astype(f32))
            hi[rows, :] = top
            lo[rows, :] = rest

        if i == 0:
            load_q.wait()
        product_p(0, i)
    pl.semaphore_wait(barrier, len(peers))
    p1_0 = scatter_first(0)
    for i in range(4):
        product_p(1, i)
    finish(p1_0)
    p2_0 = scatter_second(0)
    p1_1 = scatter_first(1)
    finish(p2_0)
    p3_0 = gather_second(0)
    finish(p1_1)
    p2_1 = scatter_second(1)
    finish(p3_0)
    p4_0 = gather_first(0)
    finish(p2_1)
    p3_1 = gather_second(1)
    finish(p3_1)
    p4_1 = gather_first(1)

    def transpose_p(s):
        for k, _ in groups(s):
            for i in range(4):
                rows = slice(256 * i, 256 * i + 256)
                top, rest = split(p_buf[k, rows, :].T)
                pt_hi[B * k : B * k + B, rows] = top
                pt_lo[B * k : B * k + B, rows] = rest

    def gram_block(s, t):
        a, b = slice(256 * s, 256 * s + 256), slice(256 * t, 256 * t + 256)
        value = mm(pt_lo[a, :], pt_lo[b, :], NT) + mm3((pt_hi[a, :], pt_lo[a, :]), (pt_hi[b, :], pt_lo[b, :]), NT)
        for n, (i, j) in enumerate(PACKED):
            if i // 2 == s and j // 2 == t:
                r, c = B * (i % 2), B * (j % 2)
                packed[B * n : B * n + B, :] = value[r : r + B, c : c + B]

    def product_w(s):
        rows = slice(256 * s, 256 * s + 256)

        def chunk(lanes):
            wt[rows, lanes] = mm3((pt_hi[rows, :], pt_lo[rows, :]), (hi[:, lanes], lo[:, lanes]), NN)

        @pl.loop(0, 6)
        def _(j):
            chunk(block(256 * j, 256))

        chunk(slice(1536, 1664))

    def ours(s):
        return block(256 * s + B * core, B)

    def theirs(s):
        return block(256 * s + B * (1 - core), B)

    pair_a, pair_b = x + 1 - 2 * (x % 2), 3 - x
    group = (x // 2, ((x + 1) // 2) % 2)
    place = (x % 2, x // 2)
    halves = (slice(0, 896), slice(896, 1664))

    def along_x(other):
        return (other * 2 + core, column)

    far = (along_x(pair_b), along_x(pair_a))
    near = (along_x(pair_a), along_x(pair_b))

    def group_rows(s, g):
        return block(256 * s + B * core + 64 * g, 64)

    def slab(s, h, i):
        return block(256 * s + B * core + 64 * group[h] + 32 * i, 32)

    def w_cores(s):
        return [send(wt.at[theirs(s)], w_recv0.at[s], other_core)]

    def w_scatter_far(s):
        wt[ours(s), :] = wt[ours(s), :] + w_recv0[s]
        return [
            send(wt.at[group_rows(s, 1 - group[h]), halves[h]], w_recv1.at[s, :, halves[h]], far[h]) for h in range(2)
        ]

    def w_scatter_near(s):
        copies = []
        for h in range(2):
            rows = group_rows(s, group[h])
            wt[rows, halves[h]] = wt[rows, halves[h]] + w_recv1[s, :, halves[h]]
            copies.append(send(wt.at[slab(s, h, 1 - place[h]), halves[h]], w_recv2.at[s, :, halves[h]], near[h]))
        return copies

    def w_gather_near(s):
        copies = []
        for h in range(2):
            mine = slab(s, h, place[h])
            w_sum[mine, halves[h]] = wt[mine, halves[h]] + w_recv2[s, :, halves[h]]
            copies.append(send(w_sum.at[mine, halves[h]], w_sum.at[mine, halves[h]], near[h]))
        return copies

    def w_gather_far(s):
        copies = []
        for h in range(2):
            rows = group_rows(s, group[h])
            copies.append(send(w_sum.at[rows, halves[h]], w_sum.at[rows, halves[h]], far[h]))
        return copies

    def w_back(s):
        return [send(w_sum.at[ours(s)], w_sum.at[ours(s)], other_core)]

    finish(p4_0)
    transpose_p(0)
    product_w(0)
    w0_0 = w_cores(0)
    gram_block(0, 0)
    finish(w0_0)
    w1_0 = w_scatter_far(0)
    finish(p4_1)
    transpose_p(1)
    gram_block(1, 0)
    gram_block(1, 1)
    g_ours, g_theirs = block(640 * core, 640), block(640 * (1 - core), 640)
    g0 = [send(packed.at[g_theirs], g_recv0, other_core)]
    finish(w1_0)
    w2_0 = w_scatter_near(0)
    finish(g0)
    packed[g_ours, :] = packed[g_ours, :] + g_recv0[...]

    def g_slab(i):
        return block(640 * core + 160 * i, 160)

    g1 = [send(packed.at[g_slab((x + d) % 4)], g_recv1.at[d - 1], at_x(d)) for d in (2, 1, 3)]
    product_w(1)
    w0_1 = w_cores(1)
    finish(g1)
    g_mine = g_slab(x)
    g_sum[g_mine, :] = (packed[g_mine, :] + g_recv1[0]) + (g_recv1[1] + g_recv1[2])
    g2 = [send(g_sum.at[g_mine], g_sum.at[g_mine], at_x(d)) for d in (2, 1, 3)]
    finish(w2_0)
    w3_0 = w_gather_near(0)
    finish(w0_1)
    w1_1 = w_scatter_far(1)
    finish(g2)
    g3 = [send(g_sum.at[g_ours], g_sum.at[g_ours], other_core)]
    inv[...] = jnp.zeros((RANK, RANK), f32)
    finish(w3_0)
    w4_0 = w_gather_far(0)
    finish(g3)
    on = lax.broadcasted_iota(jnp.int32, (B, B), 0) == lax.broadcasted_iota(jnp.int32, (B, B), 1)
    diagonals = [jnp.where(on, g_sum[B * n : B * n + B, :], 0.0) for n in (0, 2, 5, 9)]
    down = [lax.rsqrt(jnp.sum(t, axis=1, keepdims=True)) for t in diagonals]
    across = [lax.rsqrt(jnp.sum(t, axis=0, keepdims=True)) for t in diagonals]
    for n, (i, j) in enumerate(PACKED):
        gram[B * i : B * i + B, B * j : B * j + B] = g_sum[B * n : B * n + B, :] * down[i] * across[j]

    diagonal = factor_step(0, gram[0:B, 0:B], gram, inv)
    finish(w1_1)
    w2_1 = w_scatter_near(1)
    diagonal = factor_step(1, diagonal, gram, inv)
    finish(w2_1)
    w3_1 = w_gather_near(1)
    finish(w4_0)
    w5_0 = w_back(0)
    diagonal = factor_step(2, diagonal, gram, inv)
    finish(w3_1)
    w4_1 = w_gather_far(1)
    factor_step(3, diagonal, gram, inv)
    finish(w4_1)
    w5_1 = w_back(1)
    inv_hi, inv_lo = split(inv[...] * jnp.concatenate(across, axis=1))

    def right_half(rows, depth):
        squares = jnp.zeros((256, B), f32)
        for start, size in LANES:
            lanes = slice(start, start + size)
            r = mm3((inv_hi[rows, :depth], inv_lo[rows, :depth]), split(w_sum[:depth, lanes]), NN)
            r_hi[rows, lanes], r_lo[rows, lanes] = split(r)
            for i in range(0, size, B):
                squares = squares + r[:, i : i + B] * r[:, i : i + B]
        return squares

    finish(w5_0)
    upper = right_half(slice(0, 256), 256)
    finish(w5_1)
    squares = jnp.concatenate([upper, right_half(slice(256, 512), 512)], axis=0)
    saves = []

    def save(src, dst):
        copy = pltpu.make_async_copy(src, dst, save_sem.at[len(saves)])
        copy.start()
        saves.append(copy)

    save(r_hi, r_hi_hbm)
    save(r_lo, r_lo_hbm)
    col[...] = mm6(jnp.ones((8, B), f32), squares, NT)
    exchange = [send(col, col_recv.at[d - 1], at_plane(d)) for d in range(1, 16)]
    for i in range(4):
        rows = slice(256 * i, 256 * i + 256)
        p = split(jnp.concatenate([p_buf[k, rows, :] for k in range(4)], axis=1))
        orth[rows, :] = mm3(p, (inv_hi, inv_lo), NT)
    save(orth, orth_hbm)
    finish(exchange)
    total = tree([col[...]] + [col_recv[d] for d in range(15)])
    scale_ref[...] = lax.rsqrt(total * (1.0 / COLS) + epsilon)
    for copy in saves:
        copy.wait()
    for copy in started:
        copy.wait_send()


def sums(momentum, grad, q_basis):
    vmem = pl.BlockSpec(memory_space=pltpu.VMEM)
    hbm = pl.BlockSpec(memory_space=pl.ANY)
    return pl.pallas_call(
        sum_kernel,
        out_shape=[
            jax.ShapeDtypeStruct((R, RANK), f32),
            jax.ShapeDtypeStruct((RANK, C), bf16),
            jax.ShapeDtypeStruct((RANK, C), bf16),
            jax.ShapeDtypeStruct((8, RANK), f32),
        ],
        in_specs=[hbm] * 3,
        out_specs=[hbm] * 3 + [vmem],
        scratch_shapes=[
            pltpu.VMEM((R, C), f32),
            pltpu.VMEM((R, C), bf16),
            pltpu.VMEM((C, RANK), bf16),
            pltpu.VMEM((R, C), bf16),
            pltpu.VMEM((R, C), bf16),
            pltpu.VMEM((4, R, B), f32),
            pltpu.VMEM((4, 3, 256, B), f32),
            pltpu.VMEM((4, 256, B), f32),
            pltpu.VMEM((4, 3, 64, B), f32),
            pltpu.VMEM((4, R, B), f32),
            pltpu.VMEM((RANK, R), bf16),
            pltpu.VMEM((RANK, R), bf16),
            pltpu.VMEM((1280, B), f32),
            pltpu.VMEM((640, B), f32),
            pltpu.VMEM((3, 160, B), f32),
            pltpu.VMEM((1280, B), f32),
            pltpu.VMEM((RANK, RANK), f32),
            pltpu.VMEM((RANK, RANK), f32),
            pltpu.VMEM((2, B, C), f32),
            pltpu.VMEM((2, 64, C), f32),
            pltpu.VMEM((2, 32, C), f32),
            pltpu.VMEM((R, RANK), f32),
            pltpu.VMEM((8, RANK), f32),
            pltpu.VMEM((15, 8, RANK), f32),
            pltpu.SemaphoreType.DMA((9,)),
            pltpu.SemaphoreType.DMA((3,)),
            pltpu.SemaphoreType.DMA((N_MSG,)),
            pltpu.SemaphoreType.DMA((N_MSG,)),
        ],
        compiler_params=pltpu.CompilerParams(
            collective_id=0, has_side_effects=True, vmem_limit_bytes=44 << 20
        ),
        name="sums",
    )(momentum, grad, q_basis)


STEPS = 4
Q_CHUNKS = [range(13 * i // STEPS, 13 * (i + 1) // STEPS) for i in range(STEPS)]


def output_kernel(mom, grad, orth_ref, r_hi, r_lo, scale_ref, mom_out, q_out, update_out):
    scale = scale_ref[0:1, :]
    for i, chunks in enumerate(Q_CHUNKS):

        @pl.when(pl.program_id(0) == i)
        def _(chunks=chunks):
            for j in chunks:
                lanes = slice(B * j, B * j + B)
                r = r_hi[:, lanes].astype(f32) + r_lo[:, lanes].astype(f32)
                q_out[lanes, :] = (r.T * scale).astype(bf16)

    orth = orth_ref[...]
    scaled = split(orth * (scale * (float(ROWS) / RANK) ** 0.5))
    step = (orth * feedback_rate).astype(bf16)
    for start, size in LANES:
        lanes = slice(start, start + size)
        top = r_hi[:, lanes]
        merged = mom[:, lanes] + grad[:, lanes].astype(f32)
        mom_out[:, lanes] = merged - mm(step, top, NN)
        update_out[:, lanes] = mm3(scaled, (top, r_lo[:, lanes]), NN).astype(bf16)


def outputs(momentum, grad, orth, r_hi, r_lo, scale):
    whole = lambda *shape: pl.BlockSpec(shape, lambda i: (0,) * len(shape))
    slab = lambda width: pl.BlockSpec((R // STEPS, width), lambda i: (i, 0))
    return pl.pallas_call(
        output_kernel,
        grid=(STEPS,),
        out_shape=[
            jax.ShapeDtypeStruct((R, C), f32),
            jax.ShapeDtypeStruct((C, RANK), bf16),
            jax.ShapeDtypeStruct((R, C), bf16),
        ],
        in_specs=[slab(C), slab(C), slab(RANK), whole(RANK, C), whole(RANK, C), whole(8, RANK)],
        out_specs=[slab(C), whole(C, RANK), slab(C)],
        compiler_params=pltpu.CompilerParams(vmem_limit_bytes=36 << 20),
        name="outputs",
    )(momentum, grad, orth, r_hi, r_lo, scale)


def body(momentum, grad, q_basis):
    return tuple(outputs(momentum, grad, *sums(momentum, grad, q_basis)))


def solution(mesh):
    return jax.shard_map(
        body,
        mesh=mesh,
        in_specs=(P("rows", "cols"), P("rows", "cols"), P("cols", None)),
        out_specs=(P("rows", "cols"), P("cols", None), P("rows", "cols")),
        check_vma=False,
    )
```

```python
import functools

import jax
import jax.numpy as jnp
from jax import lax
from jax.experimental import pallas as pl
from jax.experimental.pallas import tpu as pltpu
from jax.sharding import PartitionSpec as P

ROWS = 8192
COLS = 26624
RANK = 512
feedback_rate = 0.05
epsilon = 1e-05

R = 1024
C = 1664
B = 128
MESH = pl.DeviceIdType.MESH
f32 = jnp.float32
bf16 = jnp.bfloat16
NN = (((1,), (0,)), ((), ()))
NT = (((1,), (1,)), ((), ()))


def mm(a, b, dims):
    return lax.dot_general(a, b, dims, preferred_element_type=f32)


def mm6(a, b, dims):
    return lax.dot_general(a, b, dims, precision=lax.Precision.HIGHEST, preferred_element_type=f32)


def split(a):
    hi = a.astype(bf16)
    return hi, (a - hi.astype(f32)).astype(bf16)


def mm3(a, b, dims):
    return mm(a[0], b[0], dims) + (mm(a[0], b[1], dims) + mm(a[1], b[0], dims))


def tree(terms):
    while len(terms) > 1:
        terms = [a + b for a, b in zip(terms[::2], terms[1::2])]
    return terms[0]


def inverse_factor(block):
    lane = lax.broadcasted_iota(jnp.int32, (8, B), 1)
    sub = lax.broadcasted_iota(jnp.int32, (8, B), 0)
    rows = [block[8 * v : 8 * v + 8, :] for v in range(16)]

    def row(x, l):
        return jnp.broadcast_to(x[l : l + 1, :], (8, B))

    def column(x, l):
        return jnp.broadcast_to(x[:, l : l + 1], (8, B))

    out = []
    for g in range(16):
        o = 8 * g
        active = (lane >= o) & (lane < o + 8)
        c = [column(rows[g], o + m) for m in range(8)]
        e = jnp.where(active, jnp.where(lane - o == sub, 1.0, 0.0), rows[g])
        e_row = [row(e, m) for m in range(8)]
        low = [jnp.where(sub == m, 1.0, 0.0) for m in range(8)]
        pivots = jnp.ones((8, B), f32)
        for l in range(0, 8, 2):
            at0, at1 = sub == l, sub == l + 1
            r = [row(c[m], l) for m in range(8)]
            s = [row(c[m], l + 1) for m in range(8)]
            p, q, t = r[l], r[l + 1], s[l + 1]
            inverse = 1.0 / (p * t - q * q)
            ratio = q / p
            pivots = jnp.where(at0, p, jnp.where(at1, t - ratio * q, pivots))
            for m in range(l):
                low[m] = jnp.where(at0, r[m], jnp.where(at1, s[m] - ratio * r[m], low[m]))
            low[l] = jnp.where(at1, -ratio, low[l])
            u = jnp.where(at0, -t, jnp.where(at1, q, t * c[l] - q * c[l + 1]))
            v = jnp.where(at0, q, jnp.where(at1, -p, p * c[l + 1] - q * c[l]))
            for m in range(8):
                if m not in (l, l + 1):
                    c[m] = jnp.where(at0 | at1, 0.0, c[m]) - (r[m] * u + s[m] * v) * inverse
            c[l], c[l + 1] = -(u * inverse), -(v * inverse)
        t = tree([low[m] * e_row[m] for m in range(8)])
        out.append(lax.rsqrt(pivots) * jnp.where(lane < o + 8, t, 0.0))
        if g == 15:
            break
        w = tree([c[m] * e_row[m] for m in range(8)])
        w_row = [row(w, m) for m in range(8)]
        for v in range(g + 1, 16):
            step = tree([column(rows[v], o + m) * w_row[m] for m in range(8)])
            rows[v] = jnp.where(active, 0.0, rows[v]) - step
    return jnp.concatenate(out, axis=0)


def factor_step(k, diagonal, gram, inv):
    o, p, n = B * k, B * (k + 1), B * (k + 2)
    x = inverse_factor(diagonal)
    inv[o:p, o:p] = x
    if k < 3:
        near = mm6(gram[p:n, o:p], x, NT)
        diagonal = gram[p:n, p:n] - mm6(near, near, NT)
    if k > 0:
        inv[o:p, 0:o] = mm6(x, inv[o:p, 0:o], NN)
    if k < 3:
        low = near
        if k < 2:
            far = mm6(gram[n:, o:p], x, NT)
            gram[n:, p:n] = gram[n:, p:n] - mm6(far, near, NT)
            gram[n:, n:] = gram[n:, n:] - mm6(far, far, NT)
            low = jnp.concatenate([near, far], axis=0)
        inv[p:, 0:p] = inv[p:, 0:p] - mm6(low, inv[o:p, 0:p], NN)
    return diagonal


PACKED = [(0, 0), (1, 0), (1, 1), (2, 0), (2, 1), (2, 2), (3, 0), (3, 1), (3, 2), (3, 3)]
LANES = [(256 * j, min(256, C - 256 * j)) for j in range(7)]
N_MSG = 159


def sum_kernel(
    mom_hbm, grad_hbm, q_hbm,
    orth_hbm, r_hi_hbm, r_lo_hbm, scale_ref,
    mom, grad, q_ref, hi, lo, part, recv1, mid, recv2, p_buf, pt_hi, pt_lo,
    packed, g_recv0, g_recv1, g_sum, gram, inv, w_recv0, w_recv1, w_recv2,
    orth, col, col_recv,
    load_sem, save_sem, send_sem, recv_sem,
):
    wt, w_sum = mom.at[0:RANK], mom.at[RANK:R]
    r_hi, r_lo = grad.at[0:RANK], grad.at[RANK:R]
    row, column = lax.axis_index("rows"), lax.axis_index("cols")
    x, core = row // 2, row % 2
    y, z = column // 4, column % 4

    def at_x(d):
        return (((x + d) % 4) * 2 + core, column)

    def at_y(d):
        return (row, ((y + d) % 4) * 4 + z)

    def at_z(d):
        return (row, y * 4 + (z + d) % 4)

    other_core = (x * 2 + 1 - core, column)

    def block(start, size):
        return pl.ds(pl.multiple_of(start, size), size)

    loads = []
    for i in range(4):
        rows = pl.ds(256 * i, 256)
        pair = [
            pltpu.make_async_copy(mom_hbm.at[rows], mom.at[rows], load_sem.at[2 * i]),
            pltpu.make_async_copy(grad_hbm.at[rows], grad.at[rows], load_sem.at[2 * i + 1]),
        ]
        for copy in pair:
            copy.start()
        loads.append(pair)
        if i == 0:
            load_q = pltpu.make_async_copy(q_hbm, q_ref, load_sem.at[8])
            load_q.start()

    barrier = pltpu.get_barrier_semaphore()

    def at_plane(d):
        return (row, (column + d) % 16)

    peers = [at_x(d) for d in (1, 2, 3)] + [at_plane(d) for d in range(1, 16)] + [other_core]
    for peer in peers:
        pl.semaphore_signal(barrier, inc=1, device_id=peer, device_id_type=MESH)

    started = []

    def send(src, dst, peer):
        number = len(started)
        copy = pltpu.make_async_remote_copy(
            src_ref=src, dst_ref=dst, send_sem=send_sem.at[number], recv_sem=recv_sem.at[number],
            device_id=peer, device_id_type=MESH,
        )
        copy.start()
        started.append(copy)
        return copy

    def finish(copies):
        for copy in copies:
            copy.wait_recv()

    at_first, at_second = (at_y, at_z), (at_z, at_y)
    first, second = (y, z), (z, y)

    def product_p(pair, i):
        rows = pl.ds(256 * i, 256)
        q = q_ref[:, 256 * pair : 256 * pair + 256]
        value = mm(hi[rows, :], q, NN) + mm(lo[rows, :], q, NN)
        part[2 * pair, rows, :] = value[:, :B]
        part[2 * pair + 1, rows, :] = value[:, B:]

    def scatter_first(s):
        copies = []
        for d in (2, 1, 3):
            for h in range(2):
                rows = block(512 * h + ((first[h] + d) % 4) * 128, 128)
                copies.append(send(part.at[s, rows], recv1.at[s, h, d - 1], at_first[h](d)))
        return copies

    def scatter_second(s):
        copies = []
        for h in range(2):
            rows = block(512 * h + first[h] * 128, 128)
            mid[s, h] = (part[s, rows, :] + recv1[s, h, 0]) + (recv1[s, h, 1] + recv1[s, h, 2])
            for d in (2, 1, 3):
                rows = block(((second[h] + d) % 4) * 32, 32)
                copies.append(send(mid.at[s, h, rows], recv2.at[s, h, d - 1], at_second[h](d)))
        return copies

    def gather_second(s):
        copies = []
        for h in range(2):
            rows = block(second[h] * 32, 32)
            mine = block(512 * h + first[h] * 128 + second[h] * 32, 32)
            p_buf[s, mine, :] = (mid[s, h, rows, :] + recv2[s, h, 0]) + (recv2[s, h, 1] + recv2[s, h, 2])
            for d in (2, 1, 3):
                copies.append(send(p_buf.at[s, mine], p_buf.at[s, mine], at_second[h](d)))
        return copies

    def gather_first(s):
        copies = []
        for h in range(2):
            mine = block(512 * h + first[h] * 128, 128)
            for d in (2, 1, 3):
                copies.append(send(p_buf.at[s, mine], p_buf.at[s, mine], at_first[h](d)))
        return copies

    for i in range(4):
        for copy in loads[i]:
            copy.wait()

        @pl.loop(0, 8)
        def _(j):
            rows = block(256 * i + 32 * j, 32)
            top, rest = split(mom[rows, :] + grad[rows, :].astype(f32))
            hi[rows, :] = top
            lo[rows, :] = rest

        if i == 0:
            load_q.wait()
        product_p(0, i)
    pl.semaphore_wait(barrier, len(peers))
    def transpose_p(s):
        for i in range(4):
            rows = slice(256 * i, 256 * i + 256)
            pt_hi[B * s : B * s + B, rows], pt_lo[B * s : B * s + B, rows] = split(p_buf[s, rows, :].T)

    def gram_block(s, t):
        a, b = slice(256 * s, 256 * s + 256), slice(256 * t, 256 * t + 256)
        value = mm(pt_lo[a, :], pt_lo[b, :], NT) + mm3((pt_hi[a, :], pt_lo[a, :]), (pt_hi[b, :], pt_lo[b, :]), NT)
        for n, (i, j) in enumerate(PACKED):
            if i // 2 == s and j // 2 == t:
                r, c = B * (i % 2), B * (j % 2)
                packed[B * n : B * n + B, :] = value[r : r + B, c : c + B]

    def product_w(s):
        rows = slice(B * s, B * s + B)

        def chunk(lanes):
            wt[rows, lanes] = mm3((pt_hi[rows, :], pt_lo[rows, :]), (hi[:, lanes], lo[:, lanes]), NN)

        @pl.loop(0, 6)
        def _(j):
            chunk(block(256 * j, 256))

        chunk(slice(1536, 1664))

    def ours(s):
        return block(B * s + 64 * core, 64)

    def theirs(s):
        return block(B * s + 64 * (1 - core), 64)

    pair_a, pair_b = x + 1 - 2 * (x % 2), 3 - x
    group = (x // 2, ((x + 1) // 2) % 2)
    place = (x % 2, x // 2)
    halves = (slice(0, 896), slice(896, 1664))

    def along_x(other):
        return (other * 2 + core, column)

    far = (along_x(pair_b), along_x(pair_a))
    near = (along_x(pair_a), along_x(pair_b))

    def group_rows(s, g):
        return block(B * s + 64 * core + 32 * g, 32)

    def slab(s, h, i):
        return block(B * s + 64 * core + 32 * group[h] + 16 * i, 16)

    def w_cores(s):
        return [send(wt.at[theirs(s)], w_recv0.at[s], other_core)]

    def w_scatter_far(s):
        wt[ours(s), :] = wt[ours(s), :] + w_recv0[s]
        return [
            send(wt.at[group_rows(s, 1 - group[h]), halves[h]], w_recv1.at[s, :, halves[h]], far[h]) for h in range(2)
        ]

    def w_scatter_near(s):
        copies = []
        for h in range(2):
            rows = group_rows(s, group[h])
            wt[rows, halves[h]] = wt[rows, halves[h]] + w_recv1[s, :, halves[h]]
            copies.append(send(wt.at[slab(s, h, 1 - place[h]), halves[h]], w_recv2.at[s, :, halves[h]], near[h]))
        return copies

    def w_gather_near(s):
        copies = []
        for h in range(2):
            mine = slab(s, h, place[h])
            w_sum[mine, halves[h]] = wt[mine, halves[h]] + w_recv2[s, :, halves[h]]
            copies.append(send(w_sum.at[mine, halves[h]], w_sum.at[mine, halves[h]], near[h]))
        return copies

    def w_gather_far(s):
        copies = []
        for h in range(2):
            rows = group_rows(s, group[h])
            copies.append(send(w_sum.at[rows, halves[h]], w_sum.at[rows, halves[h]], far[h]))
        return copies

    def w_back(s):
        return [send(w_sum.at[ours(s)], w_sum.at[ours(s)], other_core)]

    p1, p2, p3, p4 = {}, {}, {}, {}
    p1[0] = scatter_first(0)
    p1[1] = scatter_first(1)
    for i in range(4):
        product_p(1, i)
    finish(p1[0])
    p2[0] = scatter_second(0)
    p1[2] = scatter_first(2)
    finish(p1[1])
    p2[1] = scatter_second(1)
    p1[3] = scatter_first(3)
    finish(p2[0])
    p3[0] = gather_second(0)
    finish(p1[2])
    p2[2] = scatter_second(2)
    finish(p2[1])
    p3[1] = gather_second(1)
    finish(p3[0])
    p4[0] = gather_first(0)
    finish(p1[3])
    p2[3] = scatter_second(3)
    finish(p2[2])
    p3[2] = gather_second(2)
    finish(p3[1])
    p4[1] = gather_first(1)
    finish(p2[3])
    p3[3] = gather_second(3)
    finish(p3[2])
    p4[2] = gather_first(2)
    w0, w1, w2, w3, w4, w5 = {}, {}, {}, {}, {}, {}

    def start_w(s):
        product_w(s)
        w0[s] = w_cores(s)

    def scatter_far(s):
        finish(w0[s])
        w1[s] = w_scatter_far(s)

    def scatter_near(s):
        finish(w1[s])
        w2[s] = w_scatter_near(s)

    def gather_near(s):
        finish(w2[s])
        w3[s] = w_gather_near(s)

    def gather_far(s):
        finish(w3[s])
        w4[s] = w_gather_far(s)

    def gather_cores(s):
        finish(w4[s])
        w5[s] = w_back(s)

    finish(p4[0])
    transpose_p(0)
    start_w(0)
    finish(p3[3])
    p4[3] = gather_first(3)
    finish(p4[1])
    transpose_p(1)
    start_w(1)
    scatter_far(0)
    scatter_far(1)
    gram_block(0, 0)
    finish(p4[2])
    transpose_p(2)
    finish(p4[3])
    transpose_p(3)
    gram_block(1, 0)
    gram_block(1, 1)
    g_ours, g_theirs = block(640 * core, 640), block(640 * (1 - core), 640)
    g0 = [send(packed.at[g_theirs], g_recv0, other_core)]
    scatter_near(0)
    finish(g0)
    packed[g_ours, :] = packed[g_ours, :] + g_recv0[...]

    def g_slab(i):
        return block(640 * core + 160 * i, 160)

    g1 = [send(packed.at[g_slab((x + d) % 4)], g_recv1.at[d - 1], at_x(d)) for d in (2, 1, 3)]
    scatter_near(1)
    start_w(2)
    start_w(3)
    inv[...] = jnp.zeros((RANK, RANK), f32)
    finish(g1)
    g_mine = g_slab(x)
    g_sum[g_mine, :] = (packed[g_mine, :] + g_recv1[0]) + (g_recv1[1] + g_recv1[2])
    g2 = [send(g_sum.at[g_mine], g_sum.at[g_mine], at_x(d)) for d in (2, 1, 3)]
    gather_near(0)
    gather_near(1)
    finish(g2)
    g3 = [send(g_sum.at[g_ours], g_sum.at[g_ours], other_core)]
    scatter_far(2)
    scatter_far(3)
    finish(g3)
    on = lax.broadcasted_iota(jnp.int32, (B, B), 0) == lax.broadcasted_iota(jnp.int32, (B, B), 1)
    diagonals = [jnp.where(on, g_sum[B * n : B * n + B, :], 0.0) for n in (0, 2, 5, 9)]
    down = [lax.rsqrt(jnp.sum(t, axis=1, keepdims=True)) for t in diagonals]
    across = [lax.rsqrt(jnp.sum(t, axis=0, keepdims=True)) for t in diagonals]
    for n, (i, j) in enumerate(PACKED):
        gram[B * i : B * i + B, B * j : B * j + B] = g_sum[B * n : B * n + B, :] * down[i] * across[j]

    diagonal = factor_step(0, gram[0:B, 0:B], gram, inv)
    scatter_near(2)
    scatter_near(3)
    gather_far(0)
    gather_far(1)
    diagonal = factor_step(1, diagonal, gram, inv)
    gather_near(2)
    gather_near(3)
    diagonal = factor_step(2, diagonal, gram, inv)
    gather_far(2)
    gather_far(3)
    gather_cores(0)
    gather_cores(1)
    factor_step(3, diagonal, gram, inv)
    gather_cores(2)
    gather_cores(3)
    inv_hi, inv_lo = split(inv[...] * jnp.concatenate(across, axis=1))

    finish(w5[0] + w5[1])

    def keep(rows, lanes, r, squares):
        r_hi[rows, lanes], r_lo[rows, lanes] = split(r)
        for i in range(0, r.shape[1], B):
            squares = squares + r[:, i : i + B] * r[:, i : i + B]
        return squares

    first_part, last_part = slice(0, 256), slice(256, 512)
    upper = lower = jnp.zeros((256, B), f32)
    for start, size in LANES:
        lanes = slice(start, start + size)
        r = mm3((inv_hi[:, :256], inv_lo[:, :256]), split(w_sum[first_part, lanes]), NN)
        upper = keep(first_part, lanes, r[:256], upper)
        for i in range(4):
            w_recv0[i, :, lanes] = r[256 + 64 * i : 320 + 64 * i]
    finish(w5[2] + w5[3])
    for start, size in LANES:
        lanes = slice(start, start + size)
        r = mm3((inv_hi[256:, 256:], inv_lo[256:, 256:]), split(w_sum[last_part, lanes]), NN)
        r = r + jnp.concatenate([w_recv0[i, :, lanes] for i in range(4)], axis=0)
        lower = keep(last_part, lanes, r, lower)
    squares = jnp.concatenate([upper, lower], axis=0)
    saves = []

    def save(src, dst):
        copy = pltpu.make_async_copy(src, dst, save_sem.at[len(saves)])
        copy.start()
        saves.append(copy)

    save(r_hi, r_hi_hbm)
    save(r_lo, r_lo_hbm)
    col[...] = mm6(jnp.ones((8, B), f32), squares, NT)
    exchange = [send(col, col_recv.at[d - 1], at_plane(d)) for d in range(1, 16)]
    for i in range(4):
        rows = slice(256 * i, 256 * i + 256)
        p = split(jnp.concatenate([p_buf[k, rows, :] for k in range(4)], axis=1))
        orth[rows, :] = mm3(p, (inv_hi, inv_lo), NT)
    save(orth, orth_hbm)
    finish(exchange)
    total = tree([col[...]] + [col_recv[d] for d in range(15)])
    scale_ref[...] = lax.rsqrt(total * (1.0 / COLS) + epsilon)
    for copy in saves:
        copy.wait()
    for copy in started:
        copy.wait_send()


def sums(momentum, grad, q_basis):
    vmem = pl.BlockSpec(memory_space=pltpu.VMEM)
    hbm = pl.BlockSpec(memory_space=pl.ANY)
    return pl.pallas_call(
        sum_kernel,
        out_shape=[
            jax.ShapeDtypeStruct((R, RANK), f32),
            jax.ShapeDtypeStruct((RANK, C), bf16),
            jax.ShapeDtypeStruct((RANK, C), bf16),
            jax.ShapeDtypeStruct((8, RANK), f32),
        ],
        in_specs=[hbm] * 3,
        out_specs=[hbm] * 3 + [vmem],
        scratch_shapes=[
            pltpu.VMEM((R, C), f32),
            pltpu.VMEM((R, C), bf16),
            pltpu.VMEM((C, RANK), bf16),
            pltpu.VMEM((R, C), bf16),
            pltpu.VMEM((R, C), bf16),
            pltpu.VMEM((4, R, B), f32),
            pltpu.VMEM((4, 2, 3, 128, B), f32),
            pltpu.VMEM((4, 2, 128, B), f32),
            pltpu.VMEM((4, 2, 3, 32, B), f32),
            pltpu.VMEM((4, R, B), f32),
            pltpu.VMEM((RANK, R), bf16),
            pltpu.VMEM((RANK, R), bf16),
            pltpu.VMEM((1280, B), f32),
            pltpu.VMEM((640, B), f32),
            pltpu.VMEM((3, 160, B), f32),
            pltpu.VMEM((1280, B), f32),
            pltpu.VMEM((RANK, RANK), f32),
            pltpu.VMEM((RANK, RANK), f32),
            pltpu.VMEM((4, 64, C), f32),
            pltpu.VMEM((4, 32, C), f32),
            pltpu.VMEM((4, 16, C), f32),
            pltpu.VMEM((R, RANK), f32),
            pltpu.VMEM((8, RANK), f32),
            pltpu.VMEM((15, 8, RANK), f32),
            pltpu.SemaphoreType.DMA((9,)),
            pltpu.SemaphoreType.DMA((3,)),
            pltpu.SemaphoreType.DMA((N_MSG,)),
            pltpu.SemaphoreType.DMA((N_MSG,)),
        ],
        compiler_params=pltpu.CompilerParams(
            collective_id=0, has_side_effects=True, vmem_limit_bytes=44 << 20
        ),
        name="sums",
    )(momentum, grad, q_basis)


STEPS = 4
Q_CHUNKS = [range(13 * i // STEPS, 13 * (i + 1) // STEPS) for i in range(STEPS)]


def output_kernel(mom, grad, orth_ref, r_hi, r_lo, scale_ref, mom_out, q_out, update_out):
    scale = scale_ref[0:1, :]
    for i, chunks in enumerate(Q_CHUNKS):

        @pl.when(pl.program_id(0) == i)
        def _(chunks=chunks):
            for j in chunks:
                lanes = slice(B * j, B * j + B)
                r = r_hi[:, lanes].astype(f32) + r_lo[:, lanes].astype(f32)
                q_out[lanes, :] = (r.T * scale).astype(bf16)

    orth = orth_ref[...]
    scaled = split(orth * (scale * (float(ROWS) / RANK) ** 0.5))
    step = (orth * feedback_rate).astype(bf16)
    for start, size in LANES:
        lanes = slice(start, start + size)
        top = r_hi[:, lanes]
        merged = mom[:, lanes] + grad[:, lanes].astype(f32)
        mom_out[:, lanes] = merged - mm(step, top, NN)
        update_out[:, lanes] = mm3(scaled, (top, r_lo[:, lanes]), NN).astype(bf16)


def outputs(momentum, grad, orth, r_hi, r_lo, scale):
    whole = lambda *shape: pl.BlockSpec(shape, lambda i: (0,) * len(shape))
    slab = lambda width: pl.BlockSpec((R // STEPS, width), lambda i: (i, 0))
    return pl.pallas_call(
        output_kernel,
        grid=(STEPS,),
        out_shape=[
            jax.ShapeDtypeStruct((R, C), f32),
            jax.ShapeDtypeStruct((C, RANK), bf16),
            jax.ShapeDtypeStruct((R, C), bf16),
        ],
        in_specs=[slab(C), slab(C), slab(RANK), whole(RANK, C), whole(RANK, C), whole(8, RANK)],
        out_specs=[slab(C), whole(C, RANK), slab(C)],
        compiler_params=pltpu.CompilerParams(vmem_limit_bytes=36 << 20),
        name="outputs",
    )(momentum, grad, orth, r_hi, r_lo, scale)


def body(momentum, grad, q_basis):
    return tuple(outputs(momentum, grad, *sums(momentum, grad, q_basis)))


def solution(mesh):
    return jax.shard_map(
        body,
        mesh=mesh,
        in_specs=(P("rows", "cols"), P("rows", "cols"), P("cols", None)),
        out_specs=(P("rows", "cols"), P("cols", None), P("rows", "cols")),
        check_vma=False,
    )
```

```python
import functools

import jax
import jax.numpy as jnp
from jax import lax
from jax.experimental import pallas as pl
from jax.experimental.pallas import tpu as pltpu
from jax.sharding import PartitionSpec as P

ROWS = 8192
COLS = 26624
RANK = 512
feedback_rate = 0.05
epsilon = 1e-05

R = 1024
C = 1664
B = 128
MESH = pl.DeviceIdType.MESH
f32 = jnp.float32
bf16 = jnp.bfloat16
NN = (((1,), (0,)), ((), ()))
NT = (((1,), (1,)), ((), ()))


def mm(a, b, dims):
    return lax.dot_general(a, b, dims, preferred_element_type=f32)


def mm6(a, b, dims):
    return lax.dot_general(a, b, dims, precision=lax.Precision.HIGHEST, preferred_element_type=f32)


def split(a):
    hi = a.astype(bf16)
    return hi, (a - hi.astype(f32)).astype(bf16)


def mm3(a, b, dims):
    return mm(a[0], b[0], dims) + (mm(a[0], b[1], dims) + mm(a[1], b[0], dims))


def tree(terms):
    while len(terms) > 1:
        terms = [a + b for a, b in zip(terms[::2], terms[1::2])]
    return terms[0]


def inverse_factor(block):
    lane = lax.broadcasted_iota(jnp.int32, (8, B), 1)
    sub = lax.broadcasted_iota(jnp.int32, (8, B), 0)
    rows = [block[8 * v : 8 * v + 8, :] for v in range(16)]

    def row(x, l):
        return jnp.broadcast_to(x[l : l + 1, :], (8, B))

    def column(x, l):
        return jnp.broadcast_to(x[:, l : l + 1], (8, B))

    out = []
    for g in range(16):
        o = 8 * g
        active = (lane >= o) & (lane < o + 8)
        c = [column(rows[g], o + m) for m in range(8)]
        e = jnp.where(active, jnp.where(lane - o == sub, 1.0, 0.0), rows[g])
        e_row = [row(e, m) for m in range(8)]
        low = [jnp.where(sub == m, 1.0, 0.0) for m in range(8)]
        pivots = jnp.ones((8, B), f32)
        for l in range(0, 8, 2):
            at0, at1 = sub == l, sub == l + 1
            r = [row(c[m], l) for m in range(8)]
            s = [row(c[m], l + 1) for m in range(8)]
            p, q, t = r[l], r[l + 1], s[l + 1]
            inverse = 1.0 / (p * t - q * q)
            ratio = q / p
            pivots = jnp.where(at0, p, jnp.where(at1, t - ratio * q, pivots))
            for m in range(l):
                low[m] = jnp.where(at0, r[m], jnp.where(at1, s[m] - ratio * r[m], low[m]))
            low[l] = jnp.where(at1, -ratio, low[l])
            u = jnp.where(at0, -t, jnp.where(at1, q, t * c[l] - q * c[l + 1]))
            v = jnp.where(at0, q, jnp.where(at1, -p, p * c[l + 1] - q * c[l]))
            for m in range(8):
                if m not in (l, l + 1):
                    c[m] = jnp.where(at0 | at1, 0.0, c[m]) - (r[m] * u + s[m] * v) * inverse
            c[l], c[l + 1] = -(u * inverse), -(v * inverse)
        t = tree([low[m] * e_row[m] for m in range(8)])
        out.append(lax.rsqrt(pivots) * jnp.where(lane < o + 8, t, 0.0))
        if g == 15:
            break
        w = tree([c[m] * e_row[m] for m in range(8)])
        w_row = [row(w, m) for m in range(8)]
        for v in range(g + 1, 16):
            step = tree([column(rows[v], o + m) * w_row[m] for m in range(8)])
            rows[v] = jnp.where(active, 0.0, rows[v]) - step
    return jnp.concatenate(out, axis=0)


def factor_step(k, diagonal, gram, inv):
    o, p, n, end = B * k, B * (k + 1), B * (k + 2), B * 3
    x = inverse_factor(diagonal)
    inv[o:p, o:p] = x
    if k < 2:
        near = mm6(gram[p:n, o:p], x, NT)
        diagonal = gram[p:n, p:n] - mm6(near, near, NT)
    if k > 0:
        inv[o:p, 0:o] = mm6(x, inv[o:p, 0:o], NN)
    if k < 2:
        low = near
        if k == 0:
            far = mm6(gram[n:end, o:p], x, NT)
            gram[n:end, p:n] = gram[n:end, p:n] - mm6(far, near, NT)
            gram[n:end, n:end] = gram[n:end, n:end] - mm6(far, far, NT)
            low = jnp.concatenate([near, far], axis=0)
        inv[p:end, 0:p] = inv[p:end, 0:p] - mm6(low, inv[o:p, 0:p], NN)
    return diagonal


def last_step(gram, inv):
    end = B * 3
    others = inv[0:end, 0:end]
    low = mm6(gram[end:, 0:end], others, NT)
    x = inverse_factor(gram[end:, end:] - mm6(low, low, NT))
    inv[end:, end:] = x
    inv[end:, 0:end] = -mm6(x, mm6(low, others, NN), NN)


GRAM_PARTS = ((0, 768, 0, 0), (768, 512, 384, 96))
LANES = [(256 * j, min(256, C - 256 * j)) for j in range(7)]
N_MSG = 167


def sum_kernel(
    mom_hbm, grad_hbm, q_hbm,
    orth_hbm, r_hi_hbm, r_lo_hbm, scale_ref,
    mom, grad, q_ref, hi, lo, part, recv1, mid, recv2, p_buf, pt_hi, pt_lo,
    packed, g_recv0, g_recv1, g_sum, gram, inv, w_recv0, w_recv1, w_recv2,
    orth, col, col_recv,
    load_sem, save_sem, send_sem, recv_sem,
):
    wt, w_sum = mom.at[0:RANK], mom.at[RANK:R]
    r_hi, r_lo = grad.at[0:RANK], grad.at[RANK:R]
    row, column = lax.axis_index("rows"), lax.axis_index("cols")
    x, core = row // 2, row % 2
    y, z = column // 4, column % 4

    def at_x(d):
        return (((x + d) % 4) * 2 + core, column)

    def at_y(d):
        return (row, ((y + d) % 4) * 4 + z)

    def at_z(d):
        return (row, y * 4 + (z + d) % 4)

    other_core = (x * 2 + 1 - core, column)

    def block(start, size):
        return pl.ds(pl.multiple_of(start, size), size)

    loads = []
    for i in range(4):
        rows = pl.ds(256 * i, 256)
        pair = [
            pltpu.make_async_copy(mom_hbm.at[rows], mom.at[rows], load_sem.at[2 * i]),
            pltpu.make_async_copy(grad_hbm.at[rows], grad.at[rows], load_sem.at[2 * i + 1]),
        ]
        for copy in pair:
            copy.start()
        loads.append(pair)
        if i == 0:
            load_q = pltpu.make_async_copy(q_hbm, q_ref, load_sem.at[8])
            load_q.start()

    barrier = pltpu.get_barrier_semaphore()

    def at_plane(d):
        return (row, (column + d) % 16)

    peers = [at_x(d) for d in (1, 2, 3)] + [at_plane(d) for d in range(1, 16)] + [other_core]
    for peer in peers:
        pl.semaphore_signal(barrier, inc=1, device_id=peer, device_id_type=MESH)

    started = []

    def send(src, dst, peer):
        number = len(started)
        copy = pltpu.make_async_remote_copy(
            src_ref=src, dst_ref=dst, send_sem=send_sem.at[number], recv_sem=recv_sem.at[number],
            device_id=peer, device_id_type=MESH,
        )
        copy.start()
        started.append(copy)
        return copy

    def finish(copies):
        for copy in copies:
            copy.wait_recv()

    at_first, at_second = (at_y, at_z), (at_z, at_y)
    first, second = (y, z), (z, y)

    def product_p(pair, i):
        rows = pl.ds(256 * i, 256)
        q = q_ref[:, 256 * pair : 256 * pair + 256]
        value = mm(hi[rows, :], q, NN) + mm(lo[rows, :], q, NN)
        part[2 * pair, rows, :] = value[:, :B]
        part[2 * pair + 1, rows, :] = value[:, B:]

    def scatter_first(s):
        copies = []
        for d in (2, 1, 3):
            for h in range(2):
                rows = block(512 * h + ((first[h] + d) % 4) * 128, 128)
                copies.append(send(part.at[s, rows], recv1.at[s, h, d - 1], at_first[h](d)))
        return copies

    def scatter_second(s):
        copies = []
        for h in range(2):
            rows = block(512 * h + first[h] * 128, 128)
            mid[s, h] = (part[s, rows, :] + recv1[s, h, 0]) + (recv1[s, h, 1] + recv1[s, h, 2])
            for d in (2, 1, 3):
                rows = block(((second[h] + d) % 4) * 32, 32)
                copies.append(send(mid.at[s, h, rows], recv2.at[s, h, d - 1], at_second[h](d)))
        return copies

    def gather_second(s):
        copies = []
        for h in range(2):
            rows = block(second[h] * 32, 32)
            mine = block(512 * h + first[h] * 128 + second[h] * 32, 32)
            p_buf[s, mine, :] = (mid[s, h, rows, :] + recv2[s, h, 0]) + (recv2[s, h, 1] + recv2[s, h, 2])
            for d in (2, 1, 3):
                copies.append(send(p_buf.at[s, mine], p_buf.at[s, mine], at_second[h](d)))
        return copies

    def gather_first(s):
        copies = []
        for h in range(2):
            mine = block(512 * h + first[h] * 128, 128)
            for d in (2, 1, 3):
                copies.append(send(p_buf.at[s, mine], p_buf.at[s, mine], at_first[h](d)))
        return copies

    for i in range(4):
        for copy in loads[i]:
            copy.wait()

        @pl.loop(0, 8)
        def _(j):
            rows = block(256 * i + 32 * j, 32)
            top, rest = split(mom[rows, :] + grad[rows, :].astype(f32))
            hi[rows, :] = top
            lo[rows, :] = rest

        if i == 0:
            load_q.wait()
        product_p(0, i)
    pl.semaphore_wait(barrier, len(peers))
    def transpose_p(s):
        for i in range(4):
            rows = slice(256 * i, 256 * i + 256)
            pt_hi[B * s : B * s + B, rows], pt_lo[B * s : B * s + B, rows] = split(p_buf[s, rows, :].T)

    def gram_row(i):
        a, b = slice(B * i, B * i + B), slice(0, B * i + B)
        value = mm(pt_lo[a, :], pt_lo[b, :], NT) + mm3((pt_hi[a, :], pt_lo[a, :]), (pt_hi[b, :], pt_lo[b, :]), NT)
        for j in range(i + 1):
            start = B * (i * (i + 1) // 2 + j)
            packed[start : start + B, :] = value[:, B * j : B * j + B]

    def g_half(part, which):
        base, size, _, _ = GRAM_PARTS[part]
        return pl.ds(pl.multiple_of(base + which * (size // 2), 32), size // 2)

    def g_slab(part, i):
        base, size, _, _ = GRAM_PARTS[part]
        return pl.ds(pl.multiple_of(base + core * (size // 2) + i * (size // 8), 32), size // 8)

    def g_cores(part):
        _, size, at, _ = GRAM_PARTS[part]
        return [send(packed.at[g_half(part, 1 - core)], g_recv0.at[at : at + size // 2], other_core)]

    def g_scatter(part):
        _, size, at, to = GRAM_PARTS[part]
        ours = g_half(part, core)
        packed[ours, :] = packed[ours, :] + g_recv0[at : at + size // 2, :]
        return [
            send(packed.at[g_slab(part, (x + d) % 4)], g_recv1.at[d - 1, to : to + size // 8], at_x(d)) for d in (2, 1, 3)
        ]

    def g_gather(part):
        _, size, _, to = GRAM_PARTS[part]
        mine, here = g_slab(part, x), slice(to, to + size // 8)
        g_sum[mine, :] = (packed[mine, :] + g_recv1[0, here, :]) + (g_recv1[1, here, :] + g_recv1[2, here, :])
        return [send(g_sum.at[mine], g_sum.at[mine], at_x(d)) for d in (2, 1, 3)]

    def g_back(part):
        ours = g_half(part, core)
        return [send(g_sum.at[ours], g_sum.at[ours], other_core)]

    def product_w(s):
        rows = slice(B * s, B * s + B)

        def chunk(lanes):
            wt[rows, lanes] = mm3((pt_hi[rows, :], pt_lo[rows, :]), (hi[:, lanes], lo[:, lanes]), NN)

        @pl.loop(0, 6)
        def _(j):
            chunk(block(256 * j, 256))

        chunk(slice(1536, 1664))

    def ours(s):
        return block(B * s + 64 * core, 64)

    def theirs(s):
        return block(B * s + 64 * (1 - core), 64)

    pair_a, pair_b = x + 1 - 2 * (x % 2), 3 - x
    group = (x // 2, ((x + 1) // 2) % 2)
    place = (x % 2, x // 2)
    halves = (slice(0, 896), slice(896, 1664))

    def along_x(other):
        return (other * 2 + core, column)

    far = (along_x(pair_b), along_x(pair_a))
    near = (along_x(pair_a), along_x(pair_b))

    def group_rows(s, g):
        return block(B * s + 64 * core + 32 * g, 32)

    def slab(s, h, i):
        return block(B * s + 64 * core + 32 * group[h] + 16 * i, 16)

    def w_cores(s):
        return [send(wt.at[theirs(s)], w_recv0.at[s], other_core)]

    def w_scatter_far(s):
        wt[ours(s), :] = wt[ours(s), :] + w_recv0[s]
        return [
            send(wt.at[group_rows(s, 1 - group[h]), halves[h]], w_recv1.at[s, :, halves[h]], far[h]) for h in range(2)
        ]

    def w_scatter_near(s):
        copies = []
        for h in range(2):
            rows = group_rows(s, group[h])
            wt[rows, halves[h]] = wt[rows, halves[h]] + w_recv1[s, :, halves[h]]
            copies.append(send(wt.at[slab(s, h, 1 - place[h]), halves[h]], w_recv2.at[s, :, halves[h]], near[h]))
        return copies

    def w_gather_near(s):
        copies = []
        for h in range(2):
            mine = slab(s, h, place[h])
            w_sum[mine, halves[h]] = wt[mine, halves[h]] + w_recv2[s, :, halves[h]]
            copies.append(send(w_sum.at[mine, halves[h]], w_sum.at[mine, halves[h]], near[h]))
        return copies

    def w_gather_far(s):
        copies = []
        for h in range(2):
            rows = group_rows(s, group[h])
            copies.append(send(w_sum.at[rows, halves[h]], w_sum.at[rows, halves[h]], far[h]))
        return copies

    def w_back(s):
        return [send(w_sum.at[ours(s)], w_sum.at[ours(s)], other_core)]

    p1, p2, p3, p4 = {}, {}, {}, {}
    p1[0] = scatter_first(0)
    p1[1] = scatter_first(1)
    for i in range(4):
        product_p(1, i)
    finish(p1[0])
    p2[0] = scatter_second(0)
    p1[2] = scatter_first(2)
    finish(p1[1])
    p2[1] = scatter_second(1)
    p1[3] = scatter_first(3)
    finish(p2[0])
    p3[0] = gather_second(0)
    finish(p1[2])
    p2[2] = scatter_second(2)
    finish(p2[1])
    p3[1] = gather_second(1)
    finish(p3[0])
    p4[0] = gather_first(0)
    finish(p1[3])
    p2[3] = scatter_second(3)
    finish(p2[2])
    p3[2] = gather_second(2)
    finish(p3[1])
    p4[1] = gather_first(1)
    finish(p2[3])
    p3[3] = gather_second(3)
    finish(p3[2])
    p4[2] = gather_first(2)
    w0, w1, w2, w3, w4, w5 = {}, {}, {}, {}, {}, {}

    def start_w(s):
        product_w(s)
        w0[s] = w_cores(s)

    def scatter_far(s):
        finish(w0[s])
        w1[s] = w_scatter_far(s)

    def scatter_near(s):
        finish(w1[s])
        w2[s] = w_scatter_near(s)

    def gather_near(s):
        finish(w2[s])
        w3[s] = w_gather_near(s)

    def gather_far(s):
        finish(w3[s])
        w4[s] = w_gather_far(s)

    def gather_cores(s):
        finish(w4[s])
        w5[s] = w_back(s)

    on = lax.broadcasted_iota(jnp.int32, (B, B), 0) == lax.broadcasted_iota(jnp.int32, (B, B), 1)
    across = []

    def scaled_row(i):
        start = B * (i * (i + 1) // 2)
        square = jnp.where(on, g_sum[start + B * i : start + B * i + B, :], 0.0)
        down = lax.rsqrt(jnp.sum(square, axis=1, keepdims=True))
        across.append(lax.rsqrt(jnp.sum(square, axis=0, keepdims=True)))
        for j in range(i + 1):
            value = g_sum[start + B * j : start + B * j + B, :]
            gram[B * i : B * i + B, B * j : B * j + B] = value * down * across[j]

    finish(p4[0])
    transpose_p(0)
    start_w(0)
    gram_row(0)
    finish(p3[3])
    p4[3] = gather_first(3)
    finish(p4[1])
    transpose_p(1)
    start_w(1)
    scatter_far(0)
    gram_row(1)
    scatter_far(1)
    finish(p4[2])
    transpose_p(2)
    gram_row(2)
    a0 = g_cores(0)
    inv[...] = jnp.zeros((RANK, RANK), f32)
    finish(a0)
    a1 = g_scatter(0)
    finish(p4[3])
    transpose_p(3)
    gram_row(3)
    b0 = g_cores(1)
    scatter_near(0)
    finish(a1)
    a2 = g_gather(0)
    finish(b0)
    b1 = g_scatter(1)
    start_w(2)
    scatter_near(1)
    finish(a2)
    a3 = g_back(0)
    finish(b1)
    b2 = g_gather(1)
    gather_near(0)
    start_w(3)
    finish(a3)
    for i in range(3):
        scaled_row(i)
    gather_near(1)
    scatter_far(2)
    scatter_far(3)

    diagonal = factor_step(0, gram[0:B, 0:B], gram, inv)
    finish(b2)
    b3 = g_back(1)
    scatter_near(2)
    scatter_near(3)
    gather_far(0)
    gather_far(1)
    diagonal = factor_step(1, diagonal, gram, inv)
    finish(b3)
    scaled_row(3)
    gather_near(2)
    gather_near(3)
    factor_step(2, diagonal, gram, inv)
    gather_far(2)
    gather_far(3)
    gather_cores(0)
    gather_cores(1)
    last_step(gram, inv)
    gather_cores(2)
    gather_cores(3)
    inv_hi, inv_lo = split(inv[...] * jnp.concatenate(across, axis=1))

    finish(w5[0] + w5[1])

    def keep(rows, lanes, r, squares):
        r_hi[rows, lanes], r_lo[rows, lanes] = split(r)
        for i in range(0, r.shape[1], B):
            squares = squares + r[:, i : i + B] * r[:, i : i + B]
        return squares

    first_part, last_part = slice(0, 256), slice(256, 512)
    upper = lower = jnp.zeros((256, B), f32)
    for start, size in LANES:
        lanes = slice(start, start + size)
        r = mm3((inv_hi[:, :256], inv_lo[:, :256]), split(w_sum[first_part, lanes]), NN)
        upper = keep(first_part, lanes, r[:256], upper)
        for i in range(4):
            w_recv0[i, :, lanes] = r[256 + 64 * i : 320 + 64 * i]
    finish(w5[2] + w5[3])
    for start, size in LANES:
        lanes = slice(start, start + size)
        r = mm3((inv_hi[256:, 256:], inv_lo[256:, 256:]), split(w_sum[last_part, lanes]), NN)
        r = r + jnp.concatenate([w_recv0[i, :, lanes] for i in range(4)], axis=0)
        lower = keep(last_part, lanes, r, lower)
    squares = jnp.concatenate([upper, lower], axis=0)
    saves = []

    def save(src, dst):
        copy = pltpu.make_async_copy(src, dst, save_sem.at[len(saves)])
        copy.start()
        saves.append(copy)

    save(r_hi, r_hi_hbm)
    save(r_lo, r_lo_hbm)
    col[...] = mm6(jnp.ones((8, B), f32), squares, NT)
    exchange = [send(col, col_recv.at[d - 1], at_plane(d)) for d in range(1, 16)]
    for i in range(4):
        rows = slice(256 * i, 256 * i + 256)
        p = split(jnp.concatenate([p_buf[k, rows, :] for k in range(4)], axis=1))
        orth[rows, :] = mm3(p, (inv_hi, inv_lo), NT)
    save(orth, orth_hbm)
    finish(exchange)
    total = tree([col[...]] + [col_recv[d] for d in range(15)])
    scale_ref[...] = lax.rsqrt(total * (1.0 / COLS) + epsilon)
    for copy in saves:
        copy.wait()
    for copy in started:
        copy.wait_send()


def sums(momentum, grad, q_basis):
    vmem = pl.BlockSpec(memory_space=pltpu.VMEM)
    hbm = pl.BlockSpec(memory_space=pl.ANY)
    return pl.pallas_call(
        sum_kernel,
        out_shape=[
            jax.ShapeDtypeStruct((R, RANK), f32),
            jax.ShapeDtypeStruct((RANK, C), bf16),
            jax.ShapeDtypeStruct((RANK, C), bf16),
            jax.ShapeDtypeStruct((8, RANK), f32),
        ],
        in_specs=[hbm] * 3,
        out_specs=[hbm] * 3 + [vmem],
        scratch_shapes=[
            pltpu.VMEM((R, C), f32),
            pltpu.VMEM((R, C), bf16),
            pltpu.VMEM((C, RANK), bf16),
            pltpu.VMEM((R, C), bf16),
            pltpu.VMEM((R, C), bf16),
            pltpu.VMEM((4, R, B), f32),
            pltpu.VMEM((4, 2, 3, 128, B), f32),
            pltpu.VMEM((4, 2, 128, B), f32),
            pltpu.VMEM((4, 2, 3, 32, B), f32),
            pltpu.VMEM((4, R, B), f32),
            pltpu.VMEM((RANK, R), bf16),
            pltpu.VMEM((RANK, R), bf16),
            pltpu.VMEM((1280, B), f32),
            pltpu.VMEM((640, B), f32),
            pltpu.VMEM((3, 160, B), f32),
            pltpu.VMEM((1280, B), f32),
            pltpu.VMEM((RANK, RANK), f32),
            pltpu.VMEM((RANK, RANK), f32),
            pltpu.VMEM((4, 64, C), f32),
            pltpu.VMEM((4, 32, C), f32),
            pltpu.VMEM((4, 16, C), f32),
            pltpu.VMEM((R, RANK), f32),
            pltpu.VMEM((8, RANK), f32),
            pltpu.VMEM((15, 8, RANK), f32),
            pltpu.SemaphoreType.DMA((9,)),
            pltpu.SemaphoreType.DMA((3,)),
            pltpu.SemaphoreType.DMA((N_MSG,)),
            pltpu.SemaphoreType.DMA((N_MSG,)),
        ],
        compiler_params=pltpu.CompilerParams(
            collective_id=0, has_side_effects=True, vmem_limit_bytes=44 << 20
        ),
        name="sums",
    )(momentum, grad, q_basis)


STEPS = 4
Q_CHUNKS = [range(13 * i // STEPS, 13 * (i + 1) // STEPS) for i in range(STEPS)]


def output_kernel(mom, grad, orth_ref, r_hi, r_lo, scale_ref, mom_out, q_out, update_out):
    scale = scale_ref[0:1, :]
    for i, chunks in enumerate(Q_CHUNKS):

        @pl.when(pl.program_id(0) == i)
        def _(chunks=chunks):
            for j in chunks:
                lanes = slice(B * j, B * j + B)
                r = r_hi[:, lanes].astype(f32) + r_lo[:, lanes].astype(f32)
                q_out[lanes, :] = (r.T * scale).astype(bf16)

    orth = orth_ref[...]
    scaled = split(orth * (scale * (float(ROWS) / RANK) ** 0.5))
    step = (orth * feedback_rate).astype(bf16)
    for start, size in LANES:
        lanes = slice(start, start + size)
        top = r_hi[:, lanes]
        merged = mom[:, lanes] + grad[:, lanes].astype(f32)
        mom_out[:, lanes] = merged - mm(step, top, NN)
        update_out[:, lanes] = mm3(scaled, (top, r_lo[:, lanes]), NN).astype(bf16)


def outputs(momentum, grad, orth, r_hi, r_lo, scale):
    whole = lambda *shape: pl.BlockSpec(shape, lambda i: (0,) * len(shape))
    slab = lambda width: pl.BlockSpec((R // STEPS, width), lambda i: (i, 0))
    return pl.pallas_call(
        output_kernel,
        grid=(STEPS,),
        out_shape=[
            jax.ShapeDtypeStruct((R, C), f32),
            jax.ShapeDtypeStruct((C, RANK), bf16),
            jax.ShapeDtypeStruct((R, C), bf16),
        ],
        in_specs=[slab(C), slab(C), slab(RANK), whole(RANK, C), whole(RANK, C), whole(8, RANK)],
        out_specs=[slab(C), whole(C, RANK), slab(C)],
        compiler_params=pltpu.CompilerParams(vmem_limit_bytes=36 << 20),
        name="outputs",
    )(momentum, grad, orth, r_hi, r_lo, scale)


def body(momentum, grad, q_basis):
    return tuple(outputs(momentum, grad, *sums(momentum, grad, q_basis)))


def solution(mesh):
    return jax.shard_map(
        body,
        mesh=mesh,
        in_specs=(P("rows", "cols"), P("rows", "cols"), P("cols", None)),
        out_specs=(P("rows", "cols"), P("cols", None), P("rows", "cols")),
        check_vma=False,
    )
```

```python
import functools

import jax
import jax.numpy as jnp
from jax import lax
from jax.experimental import pallas as pl
from jax.experimental.pallas import tpu as pltpu
from jax.sharding import PartitionSpec as P

ROWS = 8192
COLS = 26624
RANK = 512
feedback_rate = 0.05
epsilon = 1e-05

R = 1024
C = 1664
B = 128
MESH = pl.DeviceIdType.MESH
f32 = jnp.float32
bf16 = jnp.bfloat16
NN = (((1,), (0,)), ((), ()))
NT = (((1,), (1,)), ((), ()))


def mm(a, b, dims):
    return lax.dot_general(a, b, dims, preferred_element_type=f32)


def mm6(a, b, dims):
    return lax.dot_general(a, b, dims, precision=lax.Precision.HIGHEST, preferred_element_type=f32)


def split(a):
    hi = a.astype(bf16)
    return hi, (a - hi.astype(f32)).astype(bf16)


def mm3(a, b, dims):
    return mm(a[0], b[0], dims) + (mm(a[0], b[1], dims) + mm(a[1], b[0], dims))


def tree(terms):
    while len(terms) > 1:
        terms = [a + b for a, b in zip(terms[::2], terms[1::2])]
    return terms[0]


def inverse_factor(block):
    lane = lax.broadcasted_iota(jnp.int32, (8, B), 1)
    sub = lax.broadcasted_iota(jnp.int32, (8, B), 0)
    rows = [block[8 * v : 8 * v + 8, :] for v in range(16)]

    def row(x, l):
        return jnp.broadcast_to(x[l : l + 1, :], (8, B))

    def column(x, l):
        return jnp.broadcast_to(x[:, l : l + 1], (8, B))

    out = []
    for g in range(16):
        o = 8 * g
        active = (lane >= o) & (lane < o + 8)
        c = [column(rows[g], o + m) for m in range(8)]
        e = jnp.where(active, jnp.where(lane - o == sub, 1.0, 0.0), rows[g])
        e_row = [row(e, m) for m in range(8)]
        low = [jnp.where(sub == m, 1.0, 0.0) for m in range(8)]
        pivots = jnp.ones((8, B), f32)
        for l in range(0, 8, 2):
            at0, at1 = sub == l, sub == l + 1
            r = [row(c[m], l) for m in range(8)]
            s = [row(c[m], l + 1) for m in range(8)]
            p, q, t = r[l], r[l + 1], s[l + 1]
            inverse = 1.0 / (p * t - q * q)
            ratio = q / p
            pivots = jnp.where(at0, p, jnp.where(at1, t - ratio * q, pivots))
            for m in range(l):
                low[m] = jnp.where(at0, r[m], jnp.where(at1, s[m] - ratio * r[m], low[m]))
            low[l] = jnp.where(at1, -ratio, low[l])
            u = jnp.where(at0, -t, jnp.where(at1, q, t * c[l] - q * c[l + 1]))
            v = jnp.where(at0, q, jnp.where(at1, -p, p * c[l + 1] - q * c[l]))
            for m in range(8):
                if m not in (l, l + 1):
                    c[m] = jnp.where(at0 | at1, 0.0, c[m]) - (r[m] * u + s[m] * v) * inverse
            c[l], c[l + 1] = -(u * inverse), -(v * inverse)
        t = tree([low[m] * e_row[m] for m in range(8)])
        out.append(lax.rsqrt(pivots) * jnp.where(lane < o + 8, t, 0.0))
        if g == 15:
            break
        w = tree([c[m] * e_row[m] for m in range(8)])
        w_row = [row(w, m) for m in range(8)]
        for v in range(g + 1, 16):
            step = tree([column(rows[v], o + m) * w_row[m] for m in range(8)])
            rows[v] = jnp.where(active, 0.0, rows[v]) - step
    return jnp.concatenate(out, axis=0)


def factor_step(k, diagonal, gram, inv):
    o, p, n, end = B * k, B * (k + 1), B * (k + 2), B * 3
    x = inverse_factor(diagonal)
    inv[o:p, o:p] = x
    if k < 2:
        near = mm6(gram[p:n, o:p], x, NT)
        diagonal = gram[p:n, p:n] - mm6(near, near, NT)
    if k > 0:
        inv[o:p, 0:o] = mm6(x, inv[o:p, 0:o], NN)
    if k < 2:
        low = near
        if k == 0:
            far = mm6(gram[n:end, o:p], x, NT)
            gram[n:end, p:n] = gram[n:end, p:n] - mm6(far, near, NT)
            gram[n:end, n:end] = gram[n:end, n:end] - mm6(far, far, NT)
            low = jnp.concatenate([near, far], axis=0)
        inv[p:end, 0:p] = inv[p:end, 0:p] - mm6(low, inv[o:p, 0:p], NN)
    return diagonal


def last_step(gram, inv):
    end = B * 3
    others = inv[0:end, 0:end]
    low = mm6(gram[end:, 0:end], others, NT)
    x = inverse_factor(gram[end:, end:] - mm6(low, low, NT))
    inv[end:, end:] = x
    inv[end:, 0:end] = -mm6(x, mm6(low, others, NN), NN)


GRAM_PARTS = ((0, 768, 0, 0), (768, 512, 384, 96))
LANES = [(256 * j, min(256, C - 256 * j)) for j in range(7)]
N_MSG = 167


def sum_kernel(
    mom_hbm, grad_hbm, q_hbm,
    orth_hbm, r_hi_hbm, r_lo_hbm, scale_ref,
    mom, grad, q_ref, hi, lo, part, recv1, mid, recv2, p_buf, pt_hi, pt_lo,
    packed, g_recv0, g_recv1, g_sum, gram, inv, w_recv0, w_recv1, w_recv2,
    orth, col, col_recv,
    load_sem, save_sem, send_sem, recv_sem,
):
    wt, w_sum = mom.at[0:RANK], mom.at[RANK:R]
    r_hi, r_lo = grad.at[0:RANK], grad.at[RANK:R]
    row, column = lax.axis_index("rows"), lax.axis_index("cols")
    x, core = row // 2, row % 2
    y, z = column // 4, column % 4

    def at_x(d):
        return (((x + d) % 4) * 2 + core, column)

    def at_y(d):
        return (row, ((y + d) % 4) * 4 + z)

    def at_z(d):
        return (row, y * 4 + (z + d) % 4)

    other_core = (x * 2 + 1 - core, column)

    def block(start, size):
        return pl.ds(pl.multiple_of(start, size), size)

    loads = []
    for i in range(4):
        rows = pl.ds(256 * i, 256)
        pair = [
            pltpu.make_async_copy(mom_hbm.at[rows], mom.at[rows], load_sem.at[2 * i]),
            pltpu.make_async_copy(grad_hbm.at[rows], grad.at[rows], load_sem.at[2 * i + 1]),
        ]
        for copy in pair:
            copy.start()
        loads.append(pair)
        if i == 0:
            load_q = pltpu.make_async_copy(q_hbm, q_ref, load_sem.at[8])
            load_q.start()

    barrier = pltpu.get_barrier_semaphore()

    def at_plane(d):
        return (row, (column + d) % 16)

    peers = [at_x(d) for d in (1, 2, 3)] + [at_plane(d) for d in range(1, 16)] + [other_core]
    for peer in peers:
        pl.semaphore_signal(barrier, inc=1, device_id=peer, device_id_type=MESH)

    started = []

    def send(src, dst, peer):
        number = len(started)
        copy = pltpu.make_async_remote_copy(
            src_ref=src, dst_ref=dst, send_sem=send_sem.at[number], recv_sem=recv_sem.at[number],
            device_id=peer, device_id_type=MESH,
        )
        copy.start()
        started.append(copy)
        return copy

    def finish(copies):
        for copy in copies:
            copy.wait_recv()

    at_first, at_second = (at_y, at_z), (at_z, at_y)
    first, second = (y, z), (z, y)

    def product_p(pair, i):
        rows = pl.ds(256 * i, 256)
        q = q_ref[:, 256 * pair : 256 * pair + 256]
        value = mm(hi[rows, :], q, NN) + mm(lo[rows, :], q, NN)
        part[2 * pair, rows, :] = value[:, :B]
        part[2 * pair + 1, rows, :] = value[:, B:]

    def scatter_first(s):
        copies = []
        for d in (2, 1, 3):
            for h in range(2):
                rows = block(512 * h + ((first[h] + d) % 4) * 128, 128)
                copies.append(send(part.at[s, rows], recv1.at[s, h, d - 1], at_first[h](d)))
        return copies

    def scatter_second(s):
        copies = []
        for h in range(2):
            rows = block(512 * h + first[h] * 128, 128)
            mid[s, h] = (part[s, rows, :] + recv1[s, h, 0]) + (recv1[s, h, 1] + recv1[s, h, 2])
            for d in (2, 1, 3):
                rows = block(((second[h] + d) % 4) * 32, 32)
                copies.append(send(mid.at[s, h, rows], recv2.at[s, h, d - 1], at_second[h](d)))
        return copies

    def gather_second(s):
        copies = []
        for h in range(2):
            rows = block(second[h] * 32, 32)
            mine = block(512 * h + first[h] * 128 + second[h] * 32, 32)
            p_buf[s, mine, :] = (mid[s, h, rows, :] + recv2[s, h, 0]) + (recv2[s, h, 1] + recv2[s, h, 2])
            for d in (2, 1, 3):
                copies.append(send(p_buf.at[s, mine], p_buf.at[s, mine], at_second[h](d)))
        return copies

    def gather_first(s):
        copies = []
        for h in range(2):
            mine = block(512 * h + first[h] * 128, 128)
            for d in (2, 1, 3):
                copies.append(send(p_buf.at[s, mine], p_buf.at[s, mine], at_first[h](d)))
        return copies

    for i in range(4):
        for copy in loads[i]:
            copy.wait()

        @pl.loop(0, 8)
        def _(j):
            rows = block(256 * i + 32 * j, 32)
            top, rest = split(mom[rows, :] + grad[rows, :].astype(f32))
            hi[rows, :] = top
            lo[rows, :] = rest

        if i == 0:
            load_q.wait()
        product_p(0, i)
    pl.semaphore_wait(barrier, len(peers))
    def transpose_p(s):
        for i in range(4):
            rows = slice(256 * i, 256 * i + 256)
            pt_hi[B * s : B * s + B, rows], pt_lo[B * s : B * s + B, rows] = split(p_buf[s, rows, :].T)

    def gram_row(i):
        a, b = slice(B * i, B * i + B), slice(0, B * i + B)
        value = mm(pt_lo[a, :], pt_lo[b, :], NT) + mm3((pt_hi[a, :], pt_lo[a, :]), (pt_hi[b, :], pt_lo[b, :]), NT)
        for j in range(i + 1):
            start = B * (i * (i + 1) // 2 + j)
            packed[start : start + B, :] = value[:, B * j : B * j + B]

    def g_half(part, which):
        base, size, _, _ = GRAM_PARTS[part]
        return pl.ds(pl.multiple_of(base + which * (size // 2), 32), size // 2)

    def g_slab(part, i):
        base, size, _, _ = GRAM_PARTS[part]
        return pl.ds(pl.multiple_of(base + core * (size // 2) + i * (size // 8), 32), size // 8)

    def g_cores(part):
        _, size, at, _ = GRAM_PARTS[part]
        return [send(packed.at[g_half(part, 1 - core)], g_recv0.at[at : at + size // 2], other_core)]

    def g_scatter(part):
        _, size, at, to = GRAM_PARTS[part]
        ours = g_half(part, core)
        packed[ours, :] = packed[ours, :] + g_recv0[at : at + size // 2, :]
        return [
            send(packed.at[g_slab(part, (x + d) % 4)], g_recv1.at[d - 1, to : to + size // 8], at_x(d)) for d in (2, 1, 3)
        ]

    def g_gather(part):
        _, size, _, to = GRAM_PARTS[part]
        mine, here = g_slab(part, x), slice(to, to + size // 8)
        g_sum[mine, :] = (packed[mine, :] + g_recv1[0, here, :]) + (g_recv1[1, here, :] + g_recv1[2, here, :])
        return [send(g_sum.at[mine], g_sum.at[mine], at_x(d)) for d in (2, 1, 3)]

    def g_back(part):
        ours = g_half(part, core)
        return [send(g_sum.at[ours], g_sum.at[ours], other_core)]

    def product_w(s):
        rows = slice(B * s, B * s + B)

        def chunk(lanes):
            wt[rows, lanes] = mm3((pt_hi[rows, :], pt_lo[rows, :]), (hi[:, lanes], lo[:, lanes]), NN)

        @pl.loop(0, 6)
        def _(j):
            chunk(block(256 * j, 256))

        chunk(slice(1536, 1664))

    def ours(s):
        return block(B * s + 64 * core, 64)

    def theirs(s):
        return block(B * s + 64 * (1 - core), 64)

    pair_a, pair_b = x + 1 - 2 * (x % 2), 3 - x
    group = (x // 2, ((x + 1) // 2) % 2)
    place = (x % 2, x // 2)
    halves = (slice(0, 896), slice(896, 1664))

    def along_x(other):
        return (other * 2 + core, column)

    far = (along_x(pair_b), along_x(pair_a))
    near = (along_x(pair_a), along_x(pair_b))

    def group_rows(s, g):
        return block(B * s + 64 * core + 32 * g, 32)

    def slab(s, h, i):
        return block(B * s + 64 * core + 32 * group[h] + 16 * i, 16)

    def w_cores(s):
        return [send(wt.at[theirs(s)], w_recv0.at[s], other_core)]

    def w_scatter_far(s):
        wt[ours(s), :] = wt[ours(s), :] + w_recv0[s]
        return [
            send(wt.at[group_rows(s, 1 - group[h]), halves[h]], w_recv1.at[s, :, halves[h]], far[h]) for h in range(2)
        ]

    def w_scatter_near(s):
        copies = []
        for h in range(2):
            rows = group_rows(s, group[h])
            wt[rows, halves[h]] = wt[rows, halves[h]] + w_recv1[s, :, halves[h]]
            copies.append(send(wt.at[slab(s, h, 1 - place[h]), halves[h]], w_recv2.at[s, :, halves[h]], near[h]))
        return copies

    def w_gather_near(s):
        copies = []
        for h in range(2):
            mine = slab(s, h, place[h])
            w_sum[mine, halves[h]] = wt[mine, halves[h]] + w_recv2[s, :, halves[h]]
            copies.append(send(w_sum.at[mine, halves[h]], w_sum.at[mine, halves[h]], near[h]))
        return copies

    def w_gather_far(s):
        copies = []
        for h in range(2):
            rows = group_rows(s, group[h])
            copies.append(send(w_sum.at[rows, halves[h]], w_sum.at[rows, halves[h]], far[h]))
        return copies

    def w_back(s):
        return [send(w_sum.at[ours(s)], w_sum.at[ours(s)], other_core)]

    p1, p2, p3, p4 = {}, {}, {}, {}
    p1[0] = scatter_first(0)
    p1[1] = scatter_first(1)
    for i in range(4):
        product_p(1, i)
    finish(p1[0])
    p2[0] = scatter_second(0)
    p1[2] = scatter_first(2)
    finish(p1[1])
    p2[1] = scatter_second(1)
    p1[3] = scatter_first(3)
    finish(p2[0])
    p3[0] = gather_second(0)
    finish(p1[2])
    p2[2] = scatter_second(2)
    finish(p2[1])
    p3[1] = gather_second(1)
    finish(p3[0])
    p4[0] = gather_first(0)
    finish(p1[3])
    p2[3] = scatter_second(3)
    finish(p2[2])
    p3[2] = gather_second(2)
    finish(p3[1])
    p4[1] = gather_first(1)
    finish(p2[3])
    p3[3] = gather_second(3)
    finish(p3[2])
    p4[2] = gather_first(2)
    w0, w1, w2, w3, w4, w5 = {}, {}, {}, {}, {}, {}

    def start_w(s):
        product_w(s)
        w0[s] = w_cores(s)

    def scatter_far(s):
        finish(w0[s])
        w1[s] = w_scatter_far(s)

    def scatter_near(s):
        finish(w1[s])
        w2[s] = w_scatter_near(s)

    def gather_near(s):
        finish(w2[s])
        w3[s] = w_gather_near(s)

    def gather_far(s):
        finish(w3[s])
        w4[s] = w_gather_far(s)

    def gather_cores(s):
        finish(w4[s])
        w5[s] = w_back(s)

    on = lax.broadcasted_iota(jnp.int32, (B, B), 0) == lax.broadcasted_iota(jnp.int32, (B, B), 1)
    across = []

    def scaled_row(i):
        start = B * (i * (i + 1) // 2)
        square = jnp.where(on, g_sum[start + B * i : start + B * i + B, :], 0.0)
        down = lax.rsqrt(jnp.sum(square, axis=1, keepdims=True))
        across.append(lax.rsqrt(jnp.sum(square, axis=0, keepdims=True)))
        for j in range(i + 1):
            value = g_sum[start + B * j : start + B * j + B, :]
            gram[B * i : B * i + B, B * j : B * j + B] = value * down * across[j]

    finish(p4[0])
    transpose_p(0)
    start_w(0)
    gram_row(0)
    finish(p3[3])
    p4[3] = gather_first(3)
    finish(p4[1])
    transpose_p(1)
    start_w(1)
    scatter_far(0)
    gram_row(1)
    scatter_far(1)
    finish(p4[2])
    transpose_p(2)
    gram_row(2)
    a0 = g_cores(0)
    inv[...] = jnp.zeros((RANK, RANK), f32)
    finish(a0)
    a1 = g_scatter(0)
    start_w(2)
    finish(p4[3])
    transpose_p(3)
    gram_row(3)
    b0 = g_cores(1)
    scatter_near(0)
    finish(a1)
    a2 = g_gather(0)
    finish(b0)
    b1 = g_scatter(1)
    scatter_near(1)
    finish(a2)
    a3 = g_back(0)
    finish(b1)
    b2 = g_gather(1)
    gather_near(0)
    start_w(3)
    finish(a3)
    for i in range(3):
        scaled_row(i)
    gather_near(1)
    scatter_far(2)
    scatter_far(3)

    diagonal = factor_step(0, gram[0:B, 0:B], gram, inv)
    finish(b2)
    b3 = g_back(1)
    scatter_near(2)
    scatter_near(3)
    gather_far(0)
    gather_far(1)
    diagonal = factor_step(1, diagonal, gram, inv)
    finish(b3)
    scaled_row(3)
    gather_near(2)
    gather_near(3)
    factor_step(2, diagonal, gram, inv)
    gather_far(2)
    gather_far(3)
    gather_cores(0)
    gather_cores(1)
    last_step(gram, inv)
    gather_cores(2)
    gather_cores(3)
    inv_hi, inv_lo = split(inv[...] * jnp.concatenate(across, axis=1))

    finish(w5[0] + w5[1])

    def keep(rows, lanes, r, squares):
        r_hi[rows, lanes], r_lo[rows, lanes] = split(r)
        for i in range(0, r.shape[1], B):
            squares = squares + r[:, i : i + B] * r[:, i : i + B]
        return squares

    first_part, last_part = slice(0, 256), slice(256, 512)
    upper = lower = jnp.zeros((256, B), f32)
    for start, size in LANES:
        lanes = slice(start, start + size)
        r = mm3((inv_hi[:, :256], inv_lo[:, :256]), split(w_sum[first_part, lanes]), NN)
        upper = keep(first_part, lanes, r[:256], upper)
        for i in range(4):
            w_recv0[i, :, lanes] = r[256 + 64 * i : 320 + 64 * i]
    finish(w5[2] + w5[3])
    for start, size in LANES:
        lanes = slice(start, start + size)
        r = mm3((inv_hi[256:, 256:], inv_lo[256:, 256:]), split(w_sum[last_part, lanes]), NN)
        r = r + jnp.concatenate([w_recv0[i, :, lanes] for i in range(4)], axis=0)
        lower = keep(last_part, lanes, r, lower)
    squares = jnp.concatenate([upper, lower], axis=0)
    saves = []

    def save(src, dst):
        copy = pltpu.make_async_copy(src, dst, save_sem.at[len(saves)])
        copy.start()
        saves.append(copy)

    save(r_hi, r_hi_hbm)
    save(r_lo, r_lo_hbm)
    col[...] = mm6(jnp.ones((8, B), f32), squares, NT)
    exchange = [send(col, col_recv.at[d - 1], at_plane(d)) for d in range(1, 16)]
    for i in range(4):
        rows = slice(256 * i, 256 * i + 256)
        p = split(jnp.concatenate([p_buf[k, rows, :] for k in range(4)], axis=1))
        orth[rows, :] = mm3(p, (inv_hi, inv_lo), NT)
    save(orth, orth_hbm)
    finish(exchange)
    total = tree([col[...]] + [col_recv[d] for d in range(15)])
    scale_ref[...] = lax.rsqrt(total * (1.0 / COLS) + epsilon)
    for copy in saves:
        copy.wait()
    for copy in started:
        copy.wait_send()


def sums(momentum, grad, q_basis):
    vmem = pl.BlockSpec(memory_space=pltpu.VMEM)
    hbm = pl.BlockSpec(memory_space=pl.ANY)
    return pl.pallas_call(
        sum_kernel,
        out_shape=[
            jax.ShapeDtypeStruct((R, RANK), f32),
            jax.ShapeDtypeStruct((RANK, C), bf16),
            jax.ShapeDtypeStruct((RANK, C), bf16),
            jax.ShapeDtypeStruct((8, RANK), f32),
        ],
        in_specs=[hbm] * 3,
        out_specs=[hbm] * 3 + [vmem],
        scratch_shapes=[
            pltpu.VMEM((R, C), f32),
            pltpu.VMEM((R, C), bf16),
            pltpu.VMEM((C, RANK), bf16),
            pltpu.VMEM((R, C), bf16),
            pltpu.VMEM((R, C), bf16),
            pltpu.VMEM((4, R, B), f32),
            pltpu.VMEM((4, 2, 3, 128, B), f32),
            pltpu.VMEM((4, 2, 128, B), f32),
            pltpu.VMEM((4, 2, 3, 32, B), f32),
            pltpu.VMEM((4, R, B), f32),
            pltpu.VMEM((RANK, R), bf16),
            pltpu.VMEM((RANK, R), bf16),
            pltpu.VMEM((1280, B), f32),
            pltpu.VMEM((640, B), f32),
            pltpu.VMEM((3, 160, B), f32),
            pltpu.VMEM((1280, B), f32),
            pltpu.VMEM((RANK, RANK), f32),
            pltpu.VMEM((RANK, RANK), f32),
            pltpu.VMEM((4, 64, C), f32),
            pltpu.VMEM((4, 32, C), f32),
            pltpu.VMEM((4, 16, C), f32),
            pltpu.VMEM((R, RANK), f32),
            pltpu.VMEM((8, RANK), f32),
            pltpu.VMEM((15, 8, RANK), f32),
            pltpu.SemaphoreType.DMA((9,)),
            pltpu.SemaphoreType.DMA((3,)),
            pltpu.SemaphoreType.DMA((N_MSG,)),
            pltpu.SemaphoreType.DMA((N_MSG,)),
        ],
        compiler_params=pltpu.CompilerParams(
            collective_id=0, has_side_effects=True, vmem_limit_bytes=44 << 20
        ),
        name="sums",
    )(momentum, grad, q_basis)


STEPS = 4
Q_CHUNKS = [range(13 * i // STEPS, 13 * (i + 1) // STEPS) for i in range(STEPS)]


def output_kernel(mom, grad, orth_ref, r_hi, r_lo, scale_ref, mom_out, q_out, update_out):
    scale = scale_ref[0:1, :]
    for i, chunks in enumerate(Q_CHUNKS):

        @pl.when(pl.program_id(0) == i)
        def _(chunks=chunks):
            for j in chunks:
                lanes = slice(B * j, B * j + B)
                r = r_hi[:, lanes].astype(f32) + r_lo[:, lanes].astype(f32)
                q_out[lanes, :] = (r.T * scale).astype(bf16)

    orth = orth_ref[...]
    scaled = split(orth * (scale * (float(ROWS) / RANK) ** 0.5))
    step = (orth * feedback_rate).astype(bf16)
    for start, size in LANES:
        lanes = slice(start, start + size)
        top = r_hi[:, lanes]
        merged = mom[:, lanes] + grad[:, lanes].astype(f32)
        mom_out[:, lanes] = merged - mm(step, top, NN)
        update_out[:, lanes] = mm3(scaled, (top, r_lo[:, lanes]), NN).astype(bf16)


def outputs(momentum, grad, orth, r_hi, r_lo, scale):
    whole = lambda *shape: pl.BlockSpec(shape, lambda i: (0,) * len(shape))
    slab = lambda width: pl.BlockSpec((R // STEPS, width), lambda i: (i, 0))
    return pl.pallas_call(
        output_kernel,
        grid=(STEPS,),
        out_shape=[
            jax.ShapeDtypeStruct((R, C), f32),
            jax.ShapeDtypeStruct((C, RANK), bf16),
            jax.ShapeDtypeStruct((R, C), bf16),
        ],
        in_specs=[slab(C), slab(C), slab(RANK), whole(RANK, C), whole(RANK, C), whole(8, RANK)],
        out_specs=[slab(C), whole(C, RANK), slab(C)],
        compiler_params=pltpu.CompilerParams(vmem_limit_bytes=36 << 20),
        name="outputs",
    )(momentum, grad, orth, r_hi, r_lo, scale)


def body(momentum, grad, q_basis):
    return tuple(outputs(momentum, grad, *sums(momentum, grad, q_basis)))


def solution(mesh):
    return jax.shard_map(
        body,
        mesh=mesh,
        in_specs=(P("rows", "cols"), P("rows", "cols"), P("cols", None)),
        out_specs=(P("rows", "cols"), P("cols", None), P("rows", "cols")),
        check_vma=False,
    )
```
